32 devices in a mesh: clip: 8 (over z, y), win: 4 (over x, core).
Axes of the slice: x: 2, y: 2, z: 4, core: 2. Of those that a mesh axis runs over, the one named last changes fastest.
Arguments:
- tokens: bfloat16 [16, 5120, 1024], P('clip', 'win'), may hold values from -6 to 6
- cotangent: bfloat16 [16, 5120, 1024], P('clip', 'win'), may hold values from -6 to 6
- modulation: float32 [16, 6, 1024], P('clip'), may hold values from -3 to 3
- text_features: bfloat16 [16, 77, 1024], P('clip'), may hold values from -6 to 6
- null_mask: int32 [16], P('clip'), may hold values 0 or 1
- null_text: bfloat16 [77, 1024], P(None, 'win'), may hold values from -6 to 6
- norm_gain: bfloat16 [1024], P('win'), may hold values from 0.5 to 1.5
- position_bias: float32 [16, 2025], P('win'), may hold values from -5 to 5
- self_input: bfloat16 [1024, 3072], P('clip', 'win'), may hold values from -0.1875 to 0.1875
- self_output: bfloat16 [1024, 1024], P('clip', 'win'), may hold values from -1.5 to 1.5
- cross_query: bfloat16 [1024, 1024], P('clip', 'win'), may hold values from -0.1875 to 0.1875
- cross_memory: bfloat16 [1024, 2048], P('clip', 'win'), may hold values from -0.1875 to 0.1875
- cross_output: bfloat16 [1024, 1024], P('clip', 'win'), may hold values from -1.5 to 1.5
- expand_weight: bfloat16 [1024, 4096], P('clip', 'win'), may hold values from -0.1875 to 0.1875
- reduce_weight: bfloat16 [4096, 1024], P('clip', 'win'), may hold values from -0.09375 to 0.09375
Outputs:
- block_output: bfloat16 [16, 5120, 1024], P('clip', 'win')
- tokens_grad: bfloat16 [16, 5120, 1024], P('clip', 'win')
- self_input_grad: float32 [1024, 3072], P('clip', 'win')
- self_output_grad: float32 [1024, 1024], P('clip', 'win')
- cross_query_grad: float32 [1024, 1024], P('clip', 'win')
- cross_memory_grad: float32 [1024, 2048], P('clip', 'win')
- cross_output_grad: float32 [1024, 1024], P('clip', 'win')
- expand_grad: float32 [1024, 4096], P('clip', 'win')
- reduce_grad: float32 [4096, 1024], P('clip', 'win')
- norm_gain_grad: float32 [1024], P('win')
- null_text_grad: float32 [77, 1024], P(None, 'win')
- position_bias_grad: float32 [16, 2025], P('win')
- modulation_grad: float32 [16, 6, 1024], P('clip', None, 'win')
The draws below stay inside these ranges and needn't reach their ends.
Inputs may be any that keep to these rules, and one draw needn't show every extreme that they name: `null_mask`: 1 marks a clip whose text features are replaced by the null text.
All inputs are finite; a program needn't handle non-finite values. No bound on the sum of `null_mask` on one device may be relied on, other than what follows from the above.
Results may differ from the reference program's by a relative error of at most 0.02.
Values may be sent and summed in bfloat16 or wider, within the bound.
No kernel may reach another device: no remote copies, remote signals or barrier semaphores. Data moves between devices by JAX's collectives and lax.ppermute only.
A program may use at most 448 MiB of HBM per device.

```python
import jax
import jax.numpy as jnp
from jax import lax

D = 1024
HEADS = 16
HD = 64
FF = 4096
TXT = 77
FRAMES = 5
GRID = 32
WS = 8
CLIPS = 16
SEQ = 5120
WIN_TOK = 320
NREL = 2025


def with_ends(values, key, least, largest):
    place = [jax.random.randint(jax.random.fold_in(key, axis), (), 0, length) for axis, length in enumerate(values.shape)]
    longest = values.shape.index(max(values.shape))
    neighbour = place[:longest] + [(place[longest] + 1) % values.shape[longest]] + place[longest + 1:]
    return values.at[tuple(place)].set(least).at[tuple(neighbour)].set(largest)


def steps_of(stream_key, extent, split, smallest, largest):
    factor_of = 1.0
    for axis_at, parts in split:
        draws = jax.random.uniform(jax.random.fold_in(jax.random.fold_in(stream_key, 6), axis_at), (parts,), jnp.float32, smallest / len(split), largest / len(split))
        factor_of = factor_of * jnp.repeat(jnp.exp(draws), extent[axis_at] // parts).reshape((-1,) + (1,) * (len(extent) - 1 - axis_at))
    return factor_of


def scatter_about(rng, extent, spread, bound, split=(), kind=jnp.bfloat16):
    result = jax.random.normal(rng, extent, jnp.float32) * spread
    if len(split) > 0:
        result = steps_of(rng, extent, split, -0.22, 0.18) * result
    return jnp.clip(result, min=-bound, max=bound).astype(kind)


def setup_inputs(seed: int = 0) -> dict:
    keys = jax.random.split(jax.random.key(seed), 16)
    return {
        "tokens": scatter_about(keys[0], (CLIPS, SEQ, D), 1.0, 6.0, ((0, 8), (1, 4))),
        "cotangent": scatter_about(keys[1], (CLIPS, SEQ, D), 1.0, 6.0, ((0, 8), (1, 4))),
        "modulation": scatter_about(keys[2], (CLIPS, 6, D), 0.6, 3.0, ((0, 8),), jnp.float32),
        "text_features": scatter_about(keys[3], (CLIPS, TXT, D), 1.0, 6.0, ((0, 8),)),
        "null_mask": with_ends((jax.random.randint(keys[4], (CLIPS,), 0, 2) < 1).astype(jnp.int32), jax.random.fold_in(keys[4], 1), 0, 1),
        "null_text": scatter_about(keys[5], (TXT, D), 1.0, 6.0, ((1, 4),)),
        "norm_gain": jnp.clip(1.0 + 0.1 * jax.random.normal(keys[6], (D,), jnp.float32), 0.5, 1.5).astype(jnp.bfloat16),
        "position_bias": scatter_about(keys[7], (HEADS, NREL), 1.0, 5.0, ((0, 4),), jnp.float32),
        "self_input": scatter_about(keys[8], (D, 3 * D), D ** -0.5, 0.1875, ((0, 8), (1, 4))),
        "self_output": scatter_about(keys[9], (D, D), (D // HD) ** -0.5, 1.5, ((0, 8), (1, 4))),
        "cross_query": scatter_about(keys[10], (D, D), D ** -0.5, 0.1875, ((0, 8), (1, 4))),
        "cross_memory": scatter_about(keys[11], (D, 2 * D), D ** -0.5, 0.1875, ((0, 8), (1, 4))),
        "cross_output": scatter_about(keys[12], (D, D), (D // HD) ** -0.5, 1.5, ((0, 8), (1, 4))),
        "expand_weight": scatter_about(keys[13], (D, FF), D ** -0.5, 0.1875, ((0, 8), (1, 4))),
        "reduce_weight": scatter_about(keys[14], (FF, D), FF ** -0.5, 0.09375, ((0, 8), (1, 4))),
    }


@jax.custom_vjp
def low(v):
    return lax.optimization_barrier(v.astype(jnp.bfloat16)).astype(jnp.float32)

@jax.custom_vjp
def low_back(v):
    return v

def low_keep(v):
    return (low(v), None)

def low_pass(kept, grad):
    return (grad,)

def back_keep(v):
    return (v, None)

def back_low(kept, grad):
    return (low(grad),)
low.defvjp(low_keep, low_pass)
low_back.defvjp(back_keep, back_low)
epsilon = 1e-06
gelu_coefficient = 0.7978845608028654
highest = lax.Precision.HIGHEST
group_windows = 4

def product(left, right):
    return jnp.dot(left, right, precision=highest, preferred_element_type=jnp.float32)

def normalize(values):
    centered = values - lax.optimization_barrier(jnp.mean(values, axis=-1, keepdims=True))
    variance = lax.optimization_barrier(jnp.mean(centered * centered, axis=-1, keepdims=True))
    return centered * lax.rsqrt(variance + epsilon)

def gelu_tanh(values):
    return 0.5 * values * (1.0 + jnp.tanh(gelu_coefficient * (values + 0.044715 * values * values * values)))

def softmax_last(scores):
    top_score = lax.optimization_barrier(jnp.max(scores, axis=-1, keepdims=True))
    expanded = jnp.exp(scores - top_score)
    return expanded / lax.optimization_barrier(jnp.sum(expanded, axis=-1, keepdims=True))

def relative_index():
    position = jnp.arange(WIN_TOK, dtype=jnp.int32)
    frame_index = position // (WS * WS)
    row_index = position // WS % WS
    column = position % WS
    span_width = 2 * WS - 1
    frame_part = (frame_index[:, None] - frame_index[None, :] + FRAMES - 1) * span_width
    row_part = (frame_part + row_index[:, None] - row_index[None, :] + WS - 1) * span_width
    return (row_part + column[:, None] - column[None, :] + WS - 1).astype(jnp.int32)

def clip_windows(values):
    blocks = GRID // WS
    feature_width = values.shape[-1]
    reshaped = values.reshape(FRAMES, blocks, WS, blocks, WS, feature_width)
    return reshaped.transpose(1, 3, 0, 2, 4, 5).reshape(SEQ, feature_width)

def clip_raster(values):
    blocks = GRID // WS
    feature_width = values.shape[-1]
    reshaped = values.reshape(blocks, blocks, FRAMES, WS, WS, feature_width)
    return reshaped.transpose(2, 0, 3, 1, 4, 5).reshape(SEQ, feature_width)

def clip_forward(weight_set, clip_tokens, clip_modulation, clip_text, clip_flag):
    self_input, self_output, cross_query, cross_memory, cross_output, expand_weight, reduce_weight, norm_gain, null_text, position_bias = weight_set
    scale_factor = HD ** (-0.5)
    norm_first = normalize(clip_tokens)
    hidden_first = low(norm_first * (1.0 + clip_modulation[1]) + clip_modulation[0])
    projected = low(low_back(product(hidden_first, self_input)))
    window_count = SEQ // WIN_TOK

    def grouped(columns):
        arranged = clip_windows(columns)
        return arranged.reshape(window_count // group_windows, group_windows, WIN_TOK, HEADS, HD)
    queries = grouped(projected[:, :D])
    keys_part = grouped(projected[:, D:2 * D])
    values_part = grouped(projected[:, 2 * D:])
    bias_table = jnp.take(position_bias, relative_index(), axis=1)

    def attend(group_items):
        group_queries, group_keys, group_values = group_items
        scores = jnp.einsum('wqhd,wkhd->whqk', group_queries, group_keys, precision=highest) * scale_factor
        scores = low_back(scores + bias_table[None])
        probability = low(softmax_last(scores))
        return low_back(low(jnp.einsum('whqk,wkhd->wqhd', probability, group_values, precision=highest)))
    attended = lax.map(jax.checkpoint(attend), (queries, keys_part, values_part))
    attended = clip_raster(attended.reshape(SEQ, D))
    branch = low_back(product(attended, self_output))
    first_sum = clip_tokens + clip_modulation[2] * branch
    hidden_second = low(normalize(first_sum) * norm_gain)
    used_text = jnp.where(clip_flag > 0, null_text, clip_text)
    cross_queries = low(low_back(product(hidden_second, cross_query))).reshape(SEQ, HEADS, HD)
    memory = low(product(used_text, cross_memory))
    cross_keys = memory[:, :D].reshape(TXT, HEADS, HD)
    cross_values = memory[:, D:].reshape(TXT, HEADS, HD)
    cross_scores = low_back(jnp.einsum('qhd,khd->hqk', cross_queries, cross_keys, precision=highest) * scale_factor)
    cross_probs = low(softmax_last(cross_scores))
    cross_out = low_back(low(jnp.einsum('hqk,khd->qhd', cross_probs, cross_values, precision=highest))).reshape(SEQ, D)
    second_sum = first_sum + low_back(product(cross_out, cross_output))
    hidden_third = low(normalize(second_sum) * (1.0 + clip_modulation[4]) + clip_modulation[3])
    expanded = low_back(product(hidden_third, expand_weight))
    activated = low(gelu_tanh(expanded))
    reduced = low_back(product(activated, reduce_weight))
    return second_sum + clip_modulation[5] * reduced

def reference(tokens, cotangent, modulation, text_features, null_mask, null_text, norm_gain, position_bias, self_input, self_output, cross_query, cross_memory, cross_output, expand_weight, reduce_weight):
    weight_set = tuple((weight_array.astype(jnp.float32) for weight_array in (self_input, self_output, cross_query, cross_memory, cross_output, expand_weight, reduce_weight, norm_gain, null_text, position_bias)))
    text_single = text_features.astype(jnp.float32)

    def forward(weights_in, tokens_in, modulation_in):

        def per_clip(clip_items):
            return clip_forward(weights_in, clip_items[0], clip_items[1], clip_items[2], clip_items[3])
        return lax.map(jax.checkpoint(per_clip), (tokens_in, modulation_in, text_single, null_mask))
    outputs, pullback = jax.vjp(forward, weight_set, tokens.astype(jnp.float32), modulation.astype(jnp.float32))
    weight_grads, tokens_grad, modulation_grad = pullback(cotangent.astype(jnp.float32))
    return (outputs.astype(jnp.bfloat16), tokens_grad.astype(jnp.bfloat16), weight_grads[0], weight_grads[1], weight_grads[2], weight_grads[3], weight_grads[4], weight_grads[5], weight_grads[6], weight_grads[7], weight_grads[8], weight_grads[9], modulation_grad)
```

```python
import functools

import jax
import jax.numpy as jnp
from jax import lax
from jax.experimental import pallas as pl
from jax.experimental.pallas import tpu as pltpu
from jax.sharding import PartitionSpec as P

HEADS = 16
HD = 64
FRAMES = 5
GRID = 32
WS = 8
SEQ = 5120
WIN_TOK = 320
NREL = 2025
TXT = 77
QUAD = 4
QW = QUAD * HD
QUADS = HEADS // QUAD
SPAN = 2 * WS - 1
FSPAN = 2 * FRAMES - 1
SIDE = WS * WS
PADK = 384
PADT = 128

epsilon = 1e-06
gelu_coefficient = 0.7978845608028654
scale_factor = HD ** (-0.5)
bfloat = jnp.bfloat16
single = jnp.float32
NEGATIVE = -1e30
VMEM_LIMIT = 60 * 1024 * 1024

NN = (((1,), (0,)), ((), ()))
NT = (((1,), (1,)), ((), ()))
TN = (((0,), (0,)), ((), ()))


def mm(left, right, dims=NN):
    return lax.dot_general(left, right, dims, preferred_element_type=single)


def norm_parts(values):
    centered = values - jnp.mean(values, axis=-1, keepdims=True)
    variance = jnp.mean(centered * centered, axis=-1, keepdims=True)
    inverse = lax.rsqrt(variance + epsilon)
    return centered * inverse, inverse


def norm_back(normed, inverse, grad):
    return inverse * (
        grad
        - jnp.mean(grad, axis=-1, keepdims=True)
        - normed * jnp.mean(grad * normed, axis=-1, keepdims=True)
    )


def params():
    return pltpu.CompilerParams(vmem_limit_bytes=VMEM_LIMIT)


def cost(microseconds):
    return pl.CostEstimate(
        flops=int(microseconds * 760e3),
        bytes_accessed=int(microseconds * 1e3),
        transcendentals=0,
    )


def tie(*values):
    return lax.optimization_barrier(values)


ANY = pl.BlockSpec(memory_space=pl.ANY)
PLACE = pl.BlockSpec(memory_space=pltpu.SMEM)
FIRST_ORDER = ("z", "x", "y")
OTHER_ORDER = ("z", "y", "x")


class Layout:
    def __init__(self, clip_size, win_count):
        self.clip_size, self.win_count = clip_size, win_count
        y = 2 ** ((clip_size.bit_length() - 1) // 2)
        self.size = {"z": clip_size // y, "y": y, "x": win_count // 2, "core": 2}
        self.home = {"z": "clip", "y": "clip", "x": "win", "core": "win"}
        self.stride = {"z": y, "y": 1, "x": 2, "core": 1}
        self.others = clip_size * win_count // 2

    def place(self):
        clip, win = lax.axis_index("clip"), lax.axis_index("win")
        y = self.size["y"]
        return jnp.stack([clip // y, clip % y, win // 2, win % 2]).astype(jnp.int32)

    def swap(self, values, axis, apart):
        home = self.home[axis]
        count = self.clip_size if home == "clip" else self.win_count
        step = apart * self.stride[axis]
        return lax.ppermute(values, home, [(i, i ^ step) for i in range(count)])

    def gather(self, held, order):
        held = held.reshape((-1,) + held.shape[-2:])
        for axis in order:
            apart = 1
            while apart < self.size[axis]:
                held = jnp.concatenate([held, self.swap(held, axis, apart)], axis=0)
                apart *= 2
        return held

    def owner(self, place_ref, order, index, core_apart):
        names = ("z", "y", "x", "core")
        at = {name: place_ref[i] for i, name in enumerate(names)}
        for axis in order:
            at[axis] = at[axis] ^ (index % self.size[axis])
            index = index // self.size[axis]
        core = at["core"] ^ core_apart
        return at["z"] * self.size["y"] + at["y"], at["x"] * 2 + core

    def reduce(self, term, axis, pin, first=0, last=None):
        bits = self.size[axis].bit_length() - 1
        last = bits if last is None else last
        for bit in range(first, last):
            half = term.shape[0] // 2
            part, pin = tie(self.swap(term[half:], axis, 1 << bit), pin)
            total = term[:half].astype(single) + part.astype(single)
            term = total.astype(bfloat)
        if last < bits:
            return term, pin
        return (total[0] if axis == "z" else term[0]), pin


def pack(lead, columns, *stages):
    parts = []
    for stage in stages:
        stage = stage.reshape(stage.shape[:lead] + (-1, stage.shape[-1]))
        parts += [stage[..., i : i + columns] for i in range(0, stage.shape[-1], columns)]
    return jnp.concatenate(parts, axis=lead)


def unpack(values, shapes):
    outs, at, columns = [], 0, values.shape[-1]
    for rows, cols in shapes:
        parts = []
        for _ in range(cols // columns):
            parts.append(values[at : at + rows])
            at += rows
        outs.append(jnp.concatenate(parts, axis=1))
    return outs


def reverse(index, size):
    distance, bits = 0, size.bit_length() - 1
    for b in range(bits):
        distance = distance + (((index >> b) & 1) << (bits - 1 - b))
    return distance


def start_weight(sources, target, sem, layout, place_ref, order, rows, cols, offset=0):
    depth = sources[0].shape[1]
    for apart, source in enumerate(sources):

        def step(i, carry, source=source, apart=apart):
            clip, win = layout.owner(place_ref, order, i, apart)
            for piece in range(rows // depth):
                row = pl.multiple_of(clip * rows + piece * depth, depth)
                column = pl.multiple_of(win * cols, cols)
                pltpu.make_async_copy(
                    source.at[i, :, pl.ds(offset + piece * cols, cols)],
                    target.at[pl.ds(row, depth), pl.ds(column, cols)],
                    sem,
                ).start()
            return carry

        lax.fori_loop(0, layout.others, step, 0)


def start_squares(own, other, targets, sems, layout, place_ref):
    rows, cols = own.shape[1], own.shape[2] // 3
    for i, target in enumerate(targets):
        start_weight(
            (own, other), target, sems.at[i], layout, place_ref, FIRST_ORDER, rows, cols, i * cols
        )


def start_gathered(source, target, sem, layout, cols, offset=0):
    depth = source.shape[1]
    rows = target.shape[0] // layout.clip_size

    def step(c, carry):
        for w in range(layout.win_count):
            for piece in range(rows // depth):
                row = pl.multiple_of(c * rows + piece * depth, depth)
                pltpu.make_async_copy(
                    source.at[c * layout.win_count + w, :, pl.ds(offset + piece * cols, cols)],
                    target.at[pl.ds(row, depth), pl.ds(w * cols, cols)],
                    sem,
                ).start()
        return carry

    lax.fori_loop(0, layout.clip_size, step, 0)


def wait_weight(target, sem):
    pltpu.make_async_copy(target, target, sem).wait()


def window_spec(wins, width):
    return pl.BlockSpec(
        (1, FRAMES, WS, 1, WS, width), lambda i: (i // wins, 0, 0, i % wins, 0, 0)
    )


def rows_spec(width):
    return pl.BlockSpec((1, WIN_TOK, width), lambda i: (i, 0, 0))


def modulation_spec(wins, width):
    return pl.BlockSpec((1, 6, width), lambda i: (i // wins, 0, 0))


def load_window(ref):
    return ref[0, :, :, 0].astype(single).reshape(WIN_TOK, ref.shape[-1])


def store_window(ref, values):
    ref[0, :, :, 0] = values.reshape(FRAMES, WS, WS, ref.shape[-1]).astype(ref.dtype)


def table_kernel(shift_ref, block_ref, out_ref):
    out_ref[...] = jnp.full(out_ref.shape, NEGATIVE, single)
    shift = shift_ref[0]
    for a in range(FRAMES):
        for b in range(FRAMES):
            offset = lax.rem(shift + a, FRAMES) - lax.rem(shift + b, FRAMES) + FRAMES - 1
            out_ref[0, a * SIDE : (a + 1) * SIDE, b * SIDE : (b + 1) * SIDE] = block_ref[0, offset]


def collect_kernel(shift_ref, sum_ref, out_ref):
    out_ref[...] = jnp.zeros(out_ref.shape, single)
    shift = shift_ref[0]
    for a in range(FRAMES):
        for b in range(FRAMES):
            offset = lax.rem(shift + a, FRAMES) - lax.rem(shift + b, FRAMES) + FRAMES - 1
            out_ref[0, offset] += sum_ref[0, a * SIDE : (a + 1) * SIDE, b * SIDE : (b + 1) * SIDE]


def head_spec():
    return pl.BlockSpec((1, WIN_TOK, PADK), lambda h, s: (h // QUAD, 0, h % QUAD))


def side_hot():
    shape = (SPAN * SPAN, SIDE * SIDE)
    offset = lax.broadcasted_iota(jnp.int32, shape, 0)
    pair = lax.broadcasted_iota(jnp.int32, shape, 1)
    first, second = pair // SIDE, pair % SIDE
    rows = first // WS - second // WS + WS - 1
    columns = first % WS - second % WS + WS - 1
    return (rows * SPAN + columns == offset).astype(single)


def bias_table(bias_full, shift):
    flat = bias_full.reshape(HEADS * FSPAN, SPAN * SPAN)
    blocks = jnp.dot(flat, side_hot(), precision=lax.Precision.HIGHEST)
    blocks = blocks.reshape(HEADS, FSPAN, SIDE, SIDE)
    return pl.pallas_call(
        table_kernel,
        grid_spec=pltpu.PrefetchScalarGridSpec(
            num_scalar_prefetch=1,
            grid=(HEADS,),
            in_specs=[pl.BlockSpec((1, FSPAN, SIDE, SIDE), lambda h, s: (h, 0, 0, 0))],
            out_specs=head_spec(),
        ),
        out_shape=jax.ShapeDtypeStruct((QUADS, WIN_TOK, QUAD * PADK), single),
        compiler_params=params(),
        cost_estimate=cost(12),
        name="bias_table",
    )(shift, blocks)


def bias_collect(bias_sum, shift):
    blocks = pl.pallas_call(
        collect_kernel,
        grid_spec=pltpu.PrefetchScalarGridSpec(
            num_scalar_prefetch=1,
            grid=(HEADS,),
            in_specs=[head_spec()],
            out_specs=pl.BlockSpec((1, FSPAN, SIDE, SIDE), lambda h, s: (h, 0, 0, 0)),
        ),
        out_shape=jax.ShapeDtypeStruct((HEADS, FSPAN, SIDE, SIDE), single),
        compiler_params=params(),
        cost_estimate=cost(12),
        name="bias_collect",
    )(shift, bias_sum)
    flat = blocks.reshape(HEADS * FSPAN, SIDE * SIDE)
    summed = lax.dot_general(flat, side_hot(), NT, precision=lax.Precision.HIGHEST)
    return summed.reshape(HEADS, NREL)


def project_kernel(layout, tokens_ref, mod_ref, weight_any, low_ref, out_ref, weight_ref, sem):
    @pl.when(pl.program_id(0) == 0)
    def _():
        start_gathered(weight_any, weight_ref, sem, layout, weight_any.shape[2])
        wait_weight(weight_ref, sem)

    normed, _ = norm_parts(load_window(tokens_ref))
    low = (normed * (1.0 + mod_ref[0, 1:2]) + mod_ref[0, 0:1]).astype(bfloat)
    low_ref[0] = low
    out_ref[0] = mm(low, weight_ref[...]).astype(bfloat)


def head_mask(width_rows, head):
    lane = lax.broadcasted_iota(jnp.int32, (width_rows, QW), 1)
    return (lane >= head * HD) & (lane < (head + 1) * HD)


def stacked(values, pad):
    rows = values.shape[0]
    parts = []
    for h in range(QUAD):
        parts.append(jnp.where(head_mask(rows, h), values, jnp.zeros_like(values)))
        if pad > rows:
            parts.append(jnp.zeros((pad - rows, QW), values.dtype))
    return jnp.concatenate(parts, axis=0)


def attend_kernel(q_ref, k_ref, v_ref, bias_ref, out_ref, total_ref):
    keys = stacked(k_ref[0], PADK)
    values = stacked(v_ref[0], PADK)
    queries = q_ref[0] * jnp.asarray(scale_factor, bfloat)
    scores = mm(queries, keys, NT) + bias_ref[0]
    weights = []
    for h in range(QUAD):
        part = scores[:, h * PADK : (h + 1) * PADK]
        top = jnp.max(part, axis=-1, keepdims=True)
        expanded = jnp.exp(part - top)
        total = jnp.sum(expanded, axis=-1, keepdims=True)
        weights.append((expanded * (1.0 / total)).astype(bfloat))
        total_ref[0, 0, :, h : h + 1] = top + jnp.log(total)
    out_ref[0] = mm(jnp.concatenate(weights, axis=1), values).astype(bfloat)


def attend_back_kernel(
    q_ref, k_ref, v_ref, g_ref, bias_ref, total_ref, out_ref, sum_ref
):
    @pl.when(pl.program_id(1) == 0)
    def _():
        sum_ref[...] = jnp.zeros(sum_ref.shape, single)

    keys = stacked(k_ref[0], PADK)
    values = stacked(v_ref[0], PADK)
    queries = q_ref[0] * jnp.asarray(scale_factor, bfloat)
    grad = g_ref[0]
    scores = mm(queries, keys, NT) + bias_ref[0]
    grad_probs = mm(grad, values, NT)
    queries_t = queries.T
    grad_t = grad.T
    grads, key_parts, value_parts = [], [], []
    for h in range(QUAD):
        at = slice(h * PADK, (h + 1) * PADK)
        rows = slice(h * HD, (h + 1) * HD)
        probs = jnp.exp(scores[:, at] - total_ref[0, 0, :, h : h + 1])
        gp = grad_probs[:, at]
        gs = probs * (gp - jnp.sum(probs * gp, axis=-1, keepdims=True))
        gs_low = gs.astype(bfloat)
        sum_ref[0, :, at] += gs_low.astype(single)
        grads.append(gs_low)
        key_parts.append(mm(queries_t[rows], gs_low))
        value_parts.append(mm(grad_t[rows], probs.astype(bfloat)))
    out_ref[0, 0] = (mm(jnp.concatenate(grads, axis=1), keys) * scale_factor).astype(bfloat)
    out_ref[1, 0] = jnp.concatenate(key_parts, axis=0).T[:WIN_TOK].astype(bfloat)
    out_ref[2, 0] = jnp.concatenate(value_parts, axis=0).T[:WIN_TOK].astype(bfloat)


def quad_spec(offset):
    return pl.BlockSpec((1, WIN_TOK, QW), lambda q, i: (i, 0, q + offset))


BIAS_SPEC = pl.BlockSpec((1, WIN_TOK, QUAD * PADK), lambda q, i: (q, 0, 0))
TOTAL_SPEC = pl.BlockSpec((1, 1, WIN_TOK, QUAD), lambda q, i: (q, i, 0, 0))


def memory_kernel(
    layout, place_ref, text_ref, own_any, other_any, keys_ref, values_ref, weight_ref, sem
):
    @pl.when(pl.program_id(0) == 0)
    def _():
        rows, cols = own_any.shape[1:]
        sources = (own_any, other_any)
        start_weight(sources, weight_ref, sem, layout, place_ref, OTHER_ORDER, rows, cols)
        wait_weight(weight_ref, sem)

    width = text_ref.shape[-1]
    memory = mm(text_ref[0], weight_ref[...]).astype(bfloat)
    for q in range(QUADS):
        keys_ref[0, q] = stacked(memory[:, q * QW : (q + 1) * QW], PADT)
        values_ref[0, q] = stacked(memory[:, width + q * QW : width + (q + 1) * QW], PADT)


def cross_probs(queries, keys):
    scores = mm(queries, keys, NT) * scale_factor
    lane = lax.broadcasted_iota(jnp.int32, (scores.shape[0], PADT), 1)
    parts = []
    for h in range(QUAD):
        part = jnp.where(lane < TXT, scores[:, h * PADT : (h + 1) * PADT], NEGATIVE)
        expanded = jnp.exp(part - jnp.max(part, axis=-1, keepdims=True))
        parts.append(expanded * (1.0 / jnp.sum(expanded, axis=-1, keepdims=True)))
    return parts


def cross_kernel(
    layout,
    place_ref,
    tokens_ref,
    attended_ref,
    mod_ref,
    gain_ref,
    keys_ref,
    values_ref,
    own_any,
    other_any,
    branch_ref,
    left_ref,
    queries_ref,
    sum_ref,
    output_ref,
    query_ref,
    cross_ref,
    sems,
):
    @pl.when(pl.program_id(0) == 0)
    def _():
        start_squares(own_any, other_any, (output_ref, query_ref, cross_ref), sems, layout, place_ref)
        wait_weight(output_ref, sems.at[0])
        wait_weight(query_ref, sems.at[1])
        wait_weight(cross_ref, sems.at[2])

    attended = attended_ref[0]
    left_ref[0, 0] = attended
    branch = mm(attended, output_ref[...])
    branch_ref[0] = branch
    first_sum = load_window(tokens_ref) + mod_ref[0, 2:3] * branch
    normed, _ = norm_parts(first_sum)
    second = (normed * gain_ref[...]).astype(bfloat)
    left_ref[1, 0] = second
    queries = mm(second, query_ref[...]).astype(bfloat)
    queries_ref[0] = queries
    parts = []
    for q in range(QUADS):
        probs = cross_probs(queries[:, q * QW : (q + 1) * QW], keys_ref[0, q])
        low = jnp.concatenate([p.astype(bfloat) for p in probs], axis=1)
        parts.append(mm(low, values_ref[0, q]).astype(bfloat))
    crossed = jnp.concatenate(parts, axis=1)
    left_ref[2, 0] = crossed
    sum_ref[0] = first_sum + mm(crossed, cross_ref[...])


def cross_back_kernel(
    layout,
    wins,
    place_ref,
    tokens_ref,
    mod_ref,
    gain_ref,
    keys_ref,
    values_ref,
    grad_ref,
    queries_ref,
    branch_ref,
    own_any,
    other_any,
    right_ref,
    grad_sum_ref,
    grad_attended_ref,
    memory_ref,
    gain_grad_ref,
    gate_grad_ref,
    output_ref,
    query_ref,
    cross_ref,
    sems,
):
    step = pl.program_id(0)

    @pl.when(step == 0)
    def _():
        start_squares(own_any, other_any, (output_ref, query_ref, cross_ref), sems, layout, place_ref)
        wait_weight(output_ref, sems.at[0])
        wait_weight(query_ref, sems.at[1])
        wait_weight(cross_ref, sems.at[2])
        gain_grad_ref[...] = jnp.zeros(gain_grad_ref.shape, single)

    @pl.when(step % wins == 0)
    def _():
        memory_ref[...] = jnp.zeros(memory_ref.shape, single)
        gate_grad_ref[...] = jnp.zeros(gate_grad_ref.shape, single)

    width = queries_ref.shape[-1]
    grad = grad_ref[0]
    grad_low = grad.astype(bfloat)
    right_ref[2, 0] = grad_low
    grad_crossed = mm(grad_low, cross_ref[...], NT).astype(bfloat)
    queries = queries_ref[0]
    query_parts = []
    for q in range(QUADS):
        at = slice(q * QW, (q + 1) * QW)
        probs = cross_probs(queries[:, at], keys_ref[0, q])
        grad_probs = mm(grad_crossed[:, at], values_ref[0, q], NT)
        queries_t = queries[:, at].T
        grad_t = grad_crossed[:, at].T
        grads = []
        for h in range(QUAD):
            rows = slice(h * HD, (h + 1) * HD)
            gp = grad_probs[:, h * PADT : (h + 1) * PADT]
            gs = probs[h] * (gp - jnp.sum(probs[h] * gp, axis=-1, keepdims=True))
            gs_low = gs.astype(bfloat)
            grads.append(gs_low)
            place = q * QW + h * HD
            memory_ref[0, place : place + HD] += mm(queries_t[rows], gs_low) * scale_factor
            place = width + place
            memory_ref[0, place : place + HD] += mm(grad_t[rows], probs[h].astype(bfloat))
        all_grads = jnp.concatenate(grads, axis=1)
        query_parts.append((mm(all_grads, keys_ref[0, q]) * scale_factor).astype(bfloat))
    grad_queries = jnp.concatenate(query_parts, axis=1)
    right_ref[1, 0] = grad_queries
    grad_second = mm(grad_queries, query_ref[...], NT)
    branch = branch_ref[0]
    normed, inverse = norm_parts(load_window(tokens_ref) + mod_ref[0, 2:3] * branch)
    gain_grad_ref[...] += jnp.sum(grad_second * normed, axis=0, keepdims=True)
    grad_sum = grad + norm_back(normed, inverse, grad_second * gain_ref[...])
    grad_sum_ref[0] = grad_sum
    gate_grad_ref[0] += jnp.sum(grad_sum * branch, axis=0, keepdims=True)
    grad_branch = (mod_ref[0, 2:3] * grad_sum).astype(bfloat)
    right_ref[0, 0] = grad_branch
    grad_attended_ref[0] = mm(grad_branch, output_ref[...], NT).astype(bfloat)


def null_kernel(layout, place_ref, masked_ref, own_any, other_any, out_ref, weight_ref, sem):
    rows, cols = own_any.shape[1:]
    sources = (own_any, other_any)
    start_weight(sources, weight_ref, sem, layout, place_ref, OTHER_ORDER, rows, cols)
    wait_weight(weight_ref, sem)
    masked = masked_ref[...]
    high = masked.astype(bfloat)
    rest = (masked - high.astype(single)).astype(bfloat)
    weight = weight_ref[...]
    out_ref[...] = mm(high, weight, NT) + mm(rest, weight, NT)


def null_text_term(layout, place, masked, own, other):
    width = masked.shape[1] // 2
    whole = pl.BlockSpec(memory_space=pltpu.VMEM)
    return pl.pallas_call(
        functools.partial(null_kernel, layout),
        in_specs=[PLACE, whole, ANY, ANY],
        out_specs=whole,
        out_shape=jax.ShapeDtypeStruct((masked.shape[0], width), single),
        scratch_shapes=[pltpu.VMEM((width, 2 * width), bfloat), pltpu.SemaphoreType.DMA(())],
        compiler_params=params(),
        cost_estimate=cost(5),
        name="null_text",
    )(place, masked, own, other)


def feed_kernel(
    layout,
    wins,
    chunk,
    sum_ref,
    cotangent_ref,
    mod_ref,
    weights_any,
    out_ref,
    third_ref,
    act_ref,
    grad_hidden_ref,
    grad_reduced_ref,
    grad_sum_ref,
    grad_mod_ref,
    expand_ref,
    reduce_ref,
    sems,
):
    step = pl.program_id(0)

    @pl.when(step == 0)
    def _():
        cols = expand_ref.shape[1] // layout.win_count
        start_gathered(weights_any, expand_ref, sems.at[0], layout, cols)
        offset = cols
        cols = reduce_ref.shape[1] // layout.win_count
        start_gathered(weights_any, reduce_ref, sems.at[1], layout, cols, offset)
        wait_weight(expand_ref, sems.at[0])
        wait_weight(reduce_ref, sems.at[1])

    @pl.when(step % wins == 0)
    def _():
        grad_mod_ref[...] = jnp.zeros(grad_mod_ref.shape, single)

    second_sum = sum_ref[0]
    normed, inverse = norm_parts(second_sum)
    third = (normed * (1.0 + mod_ref[0, 4:5]) + mod_ref[0, 3:4]).astype(bfloat)
    third_ref[0] = third
    grad_out = load_window(cotangent_ref)
    gate = mod_ref[0, 5:6]
    grad_reduced = (gate * grad_out).astype(bfloat)
    grad_reduced_ref[0] = grad_reduced
    hidden_width = expand_ref.shape[1]
    for at in range(0, hidden_width, chunk):
        part = slice(at, at + chunk)
        v = mm(third, expand_ref[:, part])
        grad_act = mm(grad_reduced, reduce_ref[part], NT)
        square = v * v
        tanh = jnp.tanh(gelu_coefficient * (v + 0.044715 * (square * v)))
        half = 0.5 * (1.0 + tanh)
        act_ref[0, :, part] = (v * half).astype(bfloat)
        slope = half + (0.5 * gelu_coefficient) * v * (1.0 - tanh * tanh) * (
            1.0 + (3 * 0.044715) * square
        )
        grad_hidden_ref[0, :, part] = (grad_act * slope).astype(bfloat)
    reduced = mm(act_ref[0], reduce_ref[...])
    store_window(out_ref, second_sum + gate * reduced)
    grad_third = mm(grad_hidden_ref[0], expand_ref[...], NT)
    grad_mod_ref[0, 0:1] += jnp.sum(grad_third, axis=0, keepdims=True)
    grad_mod_ref[0, 1:2] += jnp.sum(grad_third * normed, axis=0, keepdims=True)
    grad_mod_ref[0, 2:3] += jnp.sum(grad_out * reduced, axis=0, keepdims=True)
    grad_sum_ref[0] = grad_out + norm_back(normed, inverse, grad_third * (1.0 + mod_ref[0, 4:5]))


def input_back_kernel(
    layout,
    wins,
    tokens_ref,
    mod_ref,
    grad_ref,
    grad_sum_ref,
    weight_any,
    out_ref,
    grad_mod_ref,
    weight_ref,
    sem,
):
    step = pl.program_id(0)

    @pl.when(step == 0)
    def _():
        start_gathered(weight_any, weight_ref, sem, layout, weight_any.shape[2])
        wait_weight(weight_ref, sem)

    @pl.when(step % wins == 0)
    def _():
        grad_mod_ref[...] = jnp.zeros(grad_mod_ref.shape, single)

    grads = jnp.concatenate([grad_ref[0, 0], grad_ref[1, 0], grad_ref[2, 0]], axis=1)
    grad_first = mm(grads, weight_ref[...], NT)
    normed, inverse = norm_parts(load_window(tokens_ref))
    grad_mod_ref[0, 0:1] += jnp.sum(grad_first, axis=0, keepdims=True)
    grad_mod_ref[0, 1:2] += jnp.sum(grad_first * normed, axis=0, keepdims=True)
    back = norm_back(normed, inverse, grad_first * (1.0 + mod_ref[0, 1:2]))
    store_window(out_ref, grad_sum_ref[0] + back)


def owner_column(layout, place_ref, step, core_apart):
    distance = reverse(step, layout.size["x"])
    return (place_ref[2] ^ distance) * 2 + (place_ref[3] ^ core_apart)


def owner_row(layout, place_ref, y, z):
    y, z = reverse(y, layout.size["y"]), reverse(z, layout.size["z"])
    return (place_ref[0] ^ z) * layout.size["y"] + (place_ref[1] ^ y)


def columns_kernel(layout, pieces, added, x_first, place_ref, x_ref, *refs):
    y_refs, out_ref, product_ref = refs[:pieces], refs[-2], refs[-1]
    rows = out_ref.shape[-2]
    cols = out_ref.shape[-1] // pieces
    for i in range(pieces):
        product_ref[:, i * cols : (i + 1) * cols] = mm(x_ref[0], y_refs[i][0], TN)
    for y in range(layout.size["y"]):
        for z in range(layout.size["z"]):
            clip = owner_row(layout, place_ref, y, z)
            part = product_ref[pl.ds(pl.multiple_of(clip * rows, rows), rows)]
            at = (0, y, z, 0) if x_first else (y, 0, z, 0)
            if added:
                part = part + refs[pieces][at].astype(single)
            out_ref[at] = part.astype(bfloat)


def weight_grad(layout, place, x, y, pieces, core_apart, added, name, x_first=False):
    count, tokens, depth = x.shape
    width = y.shape[-1]
    unit = width // layout.win_count
    rows, cols = depth // layout.clip_size, pieces * unit
    size = layout.size

    def unit_spec(i):
        def index(n, j, place_ref):
            at = owner_column(layout, place_ref, j, core_apart) * pieces + i
            return (n * pieces + at // layout.win_count, 0, at % layout.win_count)

        return pl.BlockSpec((1, tokens, unit), index)

    if x_first:
        leading = (size["x"], size["y"], size["z"])
        block = pl.BlockSpec(
            (1,) + leading[1:] + (1, rows, cols), lambda n, j, p: (j, 0, 0, n, 0, 0)
        )
    else:
        leading = (size["y"], size["x"], size["z"])
        block = pl.BlockSpec(
            (size["y"], 1, size["z"], 1, rows, cols), lambda n, j, p: (0, j, 0, n, 0, 0)
        )
    extra = () if added is None else (added,)
    return pl.pallas_call(
        functools.partial(columns_kernel, layout, pieces, added is not None, x_first),
        grid_spec=pltpu.PrefetchScalarGridSpec(
            num_scalar_prefetch=1,
            grid=(count, size["x"]),
            in_specs=[pl.BlockSpec((1, tokens, depth), lambda n, j, p: (n, 0, 0))]
            + [unit_spec(i) for i in range(pieces)]
            + [block] * len(extra),
            out_specs=block,
            scratch_shapes=[pltpu.VMEM((depth, cols), single)],
        ),
        out_shape=jax.ShapeDtypeStruct(leading + (count, rows, cols), bfloat),
        compiler_params=params(),
        cost_estimate=cost(count * size["x"] * tokens * depth * cols / 382e3),
        name=name,
    )(place, x, *([y] * pieces), *extra)


def rows_kernel(layout, added, place_ref, x_ref, *refs):
    size = layout.size["x"]
    y_refs, out_ref = refs[:size], refs[-1]
    left = x_ref[...]
    for j in range(size):
        part = mm(left, y_refs[j][...], TN)
        if added:
            part = part + refs[size][0, j, 0].astype(single)
        out_ref[0, j, 0] = part.astype(bfloat)


def weight_grad_rows(layout, place, x, y, core_apart, added, name):
    tokens, depth = x.shape
    width = y.shape[1]
    rows, cols = depth // layout.clip_size, width // layout.win_count
    size = layout.size

    def left(y_at, z_at, place_ref):
        return (0, owner_row(layout, place_ref, y_at, z_at))

    def right(j):
        return lambda y_at, z_at, place_ref: (
            0,
            owner_column(layout, place_ref, j, core_apart),
        )

    block = pl.BlockSpec((1, size["x"], 1, rows, cols), lambda y_at, z_at, p: (y_at, 0, z_at, 0, 0))
    extra = () if added is None else (added,)
    return pl.pallas_call(
        functools.partial(rows_kernel, layout, added is not None),
        grid_spec=pltpu.PrefetchScalarGridSpec(
            num_scalar_prefetch=1,
            grid=(size["y"], size["z"]),
            in_specs=[pl.BlockSpec((tokens, rows), left)]
            + [pl.BlockSpec((tokens, cols), right(j)) for j in range(size["x"])]
            + [block] * len(extra),
            out_specs=block,
        ),
        out_shape=jax.ShapeDtypeStruct((size["y"], size["x"], size["z"], rows, cols), bfloat),
        compiler_params=params(),
        cost_estimate=cost(size["x"] * tokens * depth * cols / 382e3),
        name=name,
    )(place, x, *([y] * size["x"]), *extra)


def to_windows(values, win_count):
    clips, count, width = values.shape
    blocks = GRID // WS
    if win_count == blocks:
        chunk = WS * GRID
        parts = [values[:, k * chunk : (k + 1) * chunk] for k in range(FRAMES)]
        received = {}
        for k in range(1, blocks):
            pairs = [(w, (w + k) % win_count) for w in range(win_count)]
            received[k] = lax.ppermute(parts[k], "win", pairs)
        own = [parts[0], parts[FRAMES - 1]] + [received[k] for k in range(blocks - 1, 0, -1)]
        return jnp.stack(own, axis=1).reshape(clips, FRAMES, WS, blocks, WS, width)
    halves = win_count // blocks
    wins = blocks // halves
    me = lax.axis_index("win")
    whole = lax.all_gather(values, "win", axis=1, tiled=True)
    whole = whole.reshape(clips, FRAMES, blocks, WS, blocks, WS, width)
    whole = lax.dynamic_slice_in_dim(whole, me // halves, 1, axis=2)
    whole = lax.dynamic_slice_in_dim(whole, (me % halves) * wins, wins, axis=4)
    return whole.reshape(clips, FRAMES, WS, wins, WS, width)


def from_windows(values, win_count, pin):
    clips, _, _, wins, _, width = values.shape
    blocks = GRID // WS
    if win_count == blocks:
        chunk = WS * GRID
        parts = values.reshape(clips, FRAMES, chunk, width)
        sent = {}
        for k in range(1, blocks):
            pairs = [((w + k) % win_count, w) for w in range(win_count)]
            sent[k] = lax.ppermute(parts[:, FRAMES - k], "win", pairs)
        sent, pin = tie(sent, pin)
        own = [parts[:, 0]] + [sent[k] for k in range(1, blocks)] + [parts[:, 1]]
        return jnp.stack(own, axis=1).reshape(clips, FRAMES * chunk, width), pin
    halves = win_count // blocks
    me = lax.axis_index("win")
    whole = lax.all_gather(values, "win", axis=0, tiled=False)
    whole = whole.reshape(blocks, halves, clips, FRAMES, WS, wins, WS, width)
    whole = whole.transpose(2, 3, 0, 4, 1, 5, 6, 7).reshape(clips, SEQ, width)
    count = SEQ // win_count
    return lax.dynamic_slice_in_dim(whole, me * count, count, axis=1), pin


def gather_small(arrays, layout):
    me = lax.axis_index("win")
    held = jnp.concatenate([a.reshape(-1) for a in arrays])[None]
    apart = 1
    while apart < layout.win_count:
        came = lax.ppermute(held, "win", [(i, i ^ apart) for i in range(layout.win_count)])
        upper = (me & apart) > 0
        first, second = jnp.where(upper, came, held), jnp.where(upper, held, came)
        held = jnp.concatenate([first, second], axis=0)
        apart *= 2
    outs, at = [], 0
    for a in arrays:
        outs.append(held[:, at : at + a.size].reshape((layout.win_count,) + a.shape))
        at += a.size
    return outs


def sum_over_win(values, layout):
    me = lax.axis_index("win")
    apart = layout.win_count // 2
    while apart > 0:
        upper = (me & apart) > 0
        first, second = values[:apart], values[apart:]
        sent = jnp.where(upper, first, second)
        kept = jnp.where(upper, second, first)
        pairs = [(i, i ^ apart) for i in range(layout.win_count)]
        values = kept + lax.ppermute(sent, "win", pairs)
        apart //= 2
    return values[0]


def sum_over_clip(values, layout):
    apart = 1
    while apart < layout.clip_size:
        pairs = [(i, i ^ apart) for i in range(layout.clip_size)]
        values = values + lax.ppermute(values, "clip", pairs)
        apart *= 2
    return values


def local(
    tokens,
    cotangent,
    modulation,
    text_features,
    null_mask,
    null_text,
    norm_gain,
    position_bias,
    self_input,
    self_output,
    cross_query,
    cross_memory,
    cross_output,
    expand_weight,
    reduce_weight,
):
    win_count = lax.axis_size("win")
    clip_size = lax.axis_size("clip")
    layout = Layout(clip_size, win_count)
    place = layout.place()
    blocks = GRID // WS
    clips, _, width = tokens.shape
    hidden_width = reduce_weight.shape[0] * clip_size
    both = ("clip", "win")
    me = lax.axis_index("win")

    input_all = lax.all_gather(self_input, both, axis=0, tiled=False)
    small = [position_bias, norm_gain.astype(single), null_text.astype(single)]
    bias_full, gain_full, null_full = gather_small(small, layout)
    bias_full = bias_full.reshape(HEADS, NREL)
    tokens, bias_full = tie(tokens, bias_full)
    windowed = to_windows(tokens, win_count)
    wins = windowed.shape[3]
    windows = clips * wins
    count = windows * WIN_TOK
    columns = width // win_count
    gain_full = gain_full.reshape(1, width)
    null_full = null_full.transpose(1, 0, 2).reshape(TXT, width).astype(bfloat)
    squares = jnp.concatenate([self_output, cross_query, cross_output, cross_memory], axis=1)
    squares, bias_full = tie(squares, bias_full)
    squares_part = layout.gather(squares, ("z",))
    squares_part, windowed = tie(squares_part, windowed)
    memory_part = layout.gather(squares_part[:, :, 3 * columns :], ("y",))
    squares_part = layout.gather(squares_part[:, :, : 3 * columns], ("x",))
    depth = expand_weight.shape[0]
    feed_shard = jnp.concatenate(
        [expand_weight]
        + [reduce_weight[i : i + depth] for i in range(0, reduce_weight.shape[0], depth)],
        axis=1,
    )
    feed_all = lax.all_gather(feed_shard, both, axis=0, tiled=False)

    shift = me if win_count == blocks else jnp.int32(0)
    shift = jnp.asarray(shift, jnp.int32).reshape(1)
    table = bias_table(bias_full, shift)
    windowed, table = tie(windowed, table)

    shape = jax.ShapeDtypeStruct
    rows = functools.partial(shape, dtype=bfloat)
    wide = rows((windows, WIN_TOK, width))
    triple = rows((3, windows, WIN_TOK, width))
    triple_spec = pl.BlockSpec((3, 1, WIN_TOK, width), lambda i: (0, i, 0, 0))
    wide_single = shape((windows, WIN_TOK, width), single)
    DMA = pltpu.SemaphoreType.DMA

    first_low, projected = pl.pallas_call(
        functools.partial(project_kernel, layout),
        grid=(windows,),
        in_specs=[window_spec(wins, width), modulation_spec(wins, width), ANY],
        out_specs=[rows_spec(width), rows_spec(3 * width)],
        out_shape=[wide, rows((windows, WIN_TOK, 3 * width))],
        scratch_shapes=[pltpu.VMEM((width, 3 * width), bfloat), DMA(())],
        compiler_params=params(),
        cost_estimate=cost(26),
        name="project",
    )(windowed, modulation, input_all)
    squares_own = layout.gather(squares_part, FIRST_ORDER[2:])
    memory_own = layout.gather(memory_part, OTHER_ORDER[2:])
    squares_own, memory_own, cotangent, projected_later = tie(
        squares_own, memory_own, cotangent, projected
    )
    squares_other = layout.swap(squares_own, "core", 1)
    memory_other = layout.swap(memory_own, "core", 1)
    grad_windowed = to_windows(cotangent, win_count)

    attended, totals = pl.pallas_call(
        attend_kernel,
        grid=(QUADS, windows),
        in_specs=[quad_spec(0), quad_spec(QUADS), quad_spec(2 * QUADS), BIAS_SPEC],
        out_specs=[quad_spec(0), TOTAL_SPEC],
        out_shape=[wide, shape((QUADS, windows, WIN_TOK, QUAD), single)],
        compiler_params=params(),
        cost_estimate=cost(47),
        name="attend",
    )(projected, projected, projected, table)

    null_flags = null_mask > 0
    used_text = jnp.where(null_flags[:, None, None], null_full[None], text_features)
    text_padded = jnp.pad(used_text, ((0, 0), (0, PADT - TXT), (0, 0)))
    stack_shape = rows((clips, QUADS, QUAD * PADT, QW))
    stack_spec = pl.BlockSpec((1, QUADS, QUAD * PADT, QW), lambda i: (i, 0, 0, 0))
    cross_keys, cross_values = pl.pallas_call(
        functools.partial(memory_kernel, layout),
        grid=(clips,),
        in_specs=[PLACE, pl.BlockSpec((1, PADT, width), lambda i: (i, 0, 0)), ANY, ANY],
        out_specs=[stack_spec, stack_spec],
        out_shape=[stack_shape, stack_shape],
        scratch_shapes=[pltpu.VMEM((width, 2 * width), bfloat), DMA(())],
        compiler_params=params(),
        cost_estimate=cost(6),
        name="memory",
    )(place, text_padded, memory_own, memory_other)

    gain_spec = pl.BlockSpec((1, width), lambda i: (0, 0))
    clip_stack_spec = pl.BlockSpec((1, QUADS, QUAD * PADT, QW), lambda i: (i // wins, 0, 0, 0))
    square = pltpu.VMEM((width, width), bfloat)
    branch, lefts, cross_queries, second_sum = pl.pallas_call(
        functools.partial(cross_kernel, layout),
        grid=(windows,),
        in_specs=[
            PLACE,
            window_spec(wins, width),
            rows_spec(width),
            modulation_spec(wins, width),
            gain_spec,
            clip_stack_spec,
            clip_stack_spec,
            ANY,
            ANY,
        ],
        out_specs=[rows_spec(width), triple_spec, rows_spec(width), rows_spec(width)],
        out_shape=[wide_single, triple, wide, wide_single],
        scratch_shapes=[square, square, square, DMA((3,))],
        compiler_params=params(),
        cost_estimate=cost(42),
        name="cross",
    )(
        place,
        windowed,
        attended,
        modulation,
        gain_full,
        cross_keys,
        cross_values,
        squares_own,
        squares_other,
    )

    window_shape = rows(windowed.shape)
    block_windowed, third_low, activated, grad_hidden, grad_reduced, grad_second_sum, feed_mod = (
        pl.pallas_call(
            functools.partial(feed_kernel, layout, wins, 1024),
            grid=(windows,),
            in_specs=[
                rows_spec(width),
                window_spec(wins, width),
                modulation_spec(wins, width),
                ANY,
            ],
            out_specs=[
                window_spec(wins, width),
                rows_spec(width),
                rows_spec(hidden_width),
                rows_spec(hidden_width),
                rows_spec(width),
                rows_spec(width),
                pl.BlockSpec((1, 3, width), lambda i: (i // wins, 0, 0)),
            ],
            out_shape=[
                window_shape,
                wide,
                rows((windows, WIN_TOK, hidden_width)),
                rows((windows, WIN_TOK, hidden_width)),
                wide,
                wide_single,
                shape((clips, 3, width), single),
            ],
            scratch_shapes=[
                pltpu.VMEM((width, hidden_width), bfloat),
                pltpu.VMEM((hidden_width, width), bfloat),
                DMA((2,)),
            ],
            compiler_params=params(),
            cost_estimate=cost(117),
        name="feed",
        )(second_sum, grad_windowed, modulation, feed_all)
    )

    def flat(values):
        return values.reshape(-1, count, values.shape[-1])

    expand_of = (layout, place, flat(third_low), flat(grad_hidden), 1)
    reduce_of = (layout, place, flat(activated)[0], flat(grad_reduced)[0])
    reduce_sent = layout.swap(weight_grad_rows(*reduce_of, 1, None, "reduce_other"), "core", 1)
    expand_sent = layout.swap(weight_grad(*expand_of, 1, None, "expand_other"), "core", 1)
    reduce_term = weight_grad_rows(*reduce_of, 0, reduce_sent, "reduce_own")
    block_output, reduce_term = from_windows(block_windowed, win_count, reduce_term)
    expand_sent, reduce_term, block_output = tie(expand_sent, reduce_term, block_output)
    expand_term = weight_grad(*expand_of, 0, expand_sent, "expand_own")
    grad_second_sum, expand_term = tie(grad_second_sum, expand_term)

    rights, grad_first_sum, grad_attended, memory_t, gain_term, gate_mod = pl.pallas_call(
        functools.partial(cross_back_kernel, layout, wins),
        grid=(windows,),
        in_specs=[
            PLACE,
            window_spec(wins, width),
            modulation_spec(wins, width),
            gain_spec,
            clip_stack_spec,
            clip_stack_spec,
            rows_spec(width),
            rows_spec(width),
            rows_spec(width),
            ANY,
            ANY,
        ],
        out_specs=[
            triple_spec,
            rows_spec(width),
            rows_spec(width),
            pl.BlockSpec((1, 2 * width, PADT), lambda i: (i // wins, 0, 0)),
            gain_spec,
            pl.BlockSpec((1, 1, width), lambda i: (i // wins, 0, 0)),
        ],
        out_shape=[
            triple,
            wide_single,
            wide,
            shape((clips, 2 * width, PADT), single),
            shape((1, width), single),
            shape((clips, 1, width), single),
        ],
        scratch_shapes=[square, square, square, DMA((3,))],
        compiler_params=params(),
        cost_estimate=cost(63),
        name="cross_back",
    )(
        place,
        windowed,
        modulation,
        gain_full,
        cross_keys,
        cross_values,
        grad_second_sum,
        cross_queries,
        branch,
        squares_own,
        squares_other,
    )
    reduce_stage, grad_attended = layout.reduce(reduce_term, "y", grad_attended)
    rights, memory_t, reduce_stage = tie(rights, memory_t, reduce_stage)

    text_t = text_padded.reshape(1, clips * PADT, width)
    memory_low = memory_t.astype(bfloat).transpose(0, 2, 1).reshape(1, clips * PADT, 2 * width)
    square_of = (layout, place, flat(lefts), flat(rights), 1)
    memory_of = (layout, place, text_t, memory_low, 1)
    square_sent = layout.swap(weight_grad(*square_of, 1, None, "square_other"), "core", 1)
    memory_sent = layout.swap(weight_grad(*memory_of, 1, None, "memory_other"), "core", 1)
    expand_stage, memory_sent = layout.reduce(expand_term, "y", memory_sent)
    square_sent, memory_sent, expand_stage = tie(square_sent, memory_sent, expand_stage)
    square_term = weight_grad(*square_of, 0, square_sent, "square_own")
    memory_sent, square_term = tie(memory_sent, square_term)
    memory_term = weight_grad(*memory_of, 0, memory_sent, "memory_own")
    reduce_stage, memory_term = layout.reduce(reduce_stage, "x", memory_term)
    expand_stage, memory_term = layout.reduce(expand_stage, "x", memory_term)
    feed_stage = pack(1, columns, expand_stage, reduce_stage)
    grad_attended, feed_stage, square_term, memory_term = tie(
        grad_attended, feed_stage, square_term, memory_term
    )

    grad_projected, bias_sum = pl.pallas_call(
        attend_back_kernel,
        grid=(QUADS, windows),
        in_specs=[
            quad_spec(0),
            quad_spec(QUADS),
            quad_spec(2 * QUADS),
            quad_spec(0),
            BIAS_SPEC,
            TOTAL_SPEC,
        ],
        out_specs=[
            pl.BlockSpec((3, 1, WIN_TOK, QW), lambda q, i: (0, i, 0, q)),
            BIAS_SPEC,
        ],
        out_shape=[triple, shape((QUADS, WIN_TOK, QUAD * PADK), single)],
        compiler_params=params(),
        cost_estimate=cost(72),
        name="attend_back",
    )(projected_later, projected_later, projected_later, grad_attended, table, totals)

    input_of = (layout, place, flat(first_low), flat(grad_projected), 3)
    feed_stage, bias_sum = layout.reduce(feed_stage, "z", bias_sum, 0, 1)
    square_stage, bias_sum = layout.reduce(square_term, "y", bias_sum)
    memory_stage, bias_sum = layout.reduce(memory_term, "y", bias_sum)
    rest_stage = pack(2, columns, square_stage, memory_stage)
    grad_projected, rest_stage, feed_stage = tie(grad_projected, rest_stage, feed_stage)
    input_of = (layout, place, flat(first_low), flat(grad_projected), 3)
    input_sent = weight_grad(*input_of, 1, None, "input_other", True)
    masked = jnp.sum(jnp.where(null_flags[:, None, None], memory_t[:, :, :TXT], 0.0), axis=0)
    masked = jnp.pad(masked.T, ((0, 128 - TXT), (0, 0)))
    input_sent, masked = tie(input_sent, masked)
    input_sent = layout.swap(input_sent, "core", 1)
    null_term = null_text_term(layout, place, masked, memory_own, memory_other)[:TXT]
    input_sent, null_term = tie(input_sent, null_term)
    input_term = weight_grad(*input_of, 0, input_sent, "input_own", True)
    feed_grad, input_term = layout.reduce(feed_stage, "z", input_term, 1)
    rest_stage, input_term = layout.reduce(rest_stage, "x", input_term)
    grad_projected, rest_stage, feed_grad, input_term = tie(
        grad_projected, rest_stage, feed_grad, input_term
    )

    tokens_windowed, first_mod = pl.pallas_call(
        functools.partial(input_back_kernel, layout, wins),
        grid=(windows,),
        in_specs=[
            window_spec(wins, width),
            modulation_spec(wins, width),
            triple_spec,
            rows_spec(width),
            ANY,
        ],
        out_specs=[
            window_spec(wins, width),
            pl.BlockSpec((1, 2, width), lambda i: (i // wins, 0, 0)),
        ],
        out_shape=[window_shape, shape((clips, 2, width), single)],
        scratch_shapes=[pltpu.VMEM((width, 3 * width), bfloat), DMA(())],
        compiler_params=params(),
        cost_estimate=cost(29),
        name="input_back",
    )(windowed, modulation, grad_projected, grad_first_sum, input_all)
    rest_grad, tokens_windowed = layout.reduce(rest_stage, "z", tokens_windowed)
    input_stage, tokens_windowed = layout.reduce(input_term, "x", tokens_windowed)
    bias_sum, tokens_windowed = tie(bias_sum, tokens_windowed)
    tokens_grad, _ = from_windows(tokens_windowed, win_count, None)
    input_stage, _ = layout.reduce(input_stage, "y", None)
    self_input_grad = layout.reduce(input_stage, "z", None)[0][0]
    expand_grad, reduce_grad = unpack(feed_grad, ((depth, 4 * columns), (4 * depth, columns)))
    square_grads, cross_memory_grad = unpack(
        rest_grad, ((3 * depth, columns), (depth, 2 * columns))
    )
    square_grads = square_grads.reshape(3, depth, columns)
    heads_local = HEADS // win_count
    position_term = bias_collect(bias_sum, shift)
    modulation_term = jnp.concatenate([first_mod, gate_mod, feed_mod], axis=1)
    by_columns = jnp.concatenate(
        [modulation_term.reshape(clips * 6, width), gain_term, null_term], axis=0
    )
    by_columns = by_columns.reshape(-1, win_count, columns).transpose(1, 0, 2)
    small_term = jnp.concatenate(
        [
            by_columns.reshape(win_count, -1),
            position_term.reshape(win_count, heads_local * NREL),
        ],
        axis=1,
    )
    small_term = sum_over_win(small_term, layout)
    modulation_grad = small_term[: clips * 6 * columns].reshape(clips, 6, columns)
    small_grad = sum_over_clip(small_term[clips * 6 * columns :], layout)
    gain_grad = small_grad[:columns]
    null_grad = small_grad[columns : (1 + TXT) * columns].reshape(TXT, columns)
    position_grad = small_grad[(1 + TXT) * columns :].reshape(heads_local, NREL)
    self_output_grad, cross_query_grad, cross_output_grad = square_grads
    return (
        block_output,
        tokens_grad,
        self_input_grad,
        self_output_grad,
        cross_query_grad,
        cross_memory_grad,
        cross_output_grad,
        expand_grad,
        reduce_grad,
        gain_grad,
        null_grad,
        position_grad,
        modulation_grad,
    )


def solution(mesh):
    in_specs = (
        P("clip", "win", None),
        P("clip", "win", None),
        P("clip", None, None),
        P("clip", None, None),
        P("clip"),
        P(None, "win"),
        P("win"),
        P("win", None),
        P("clip", "win"),
        P("clip", "win"),
        P("clip", "win"),
        P("clip", "win"),
        P("clip", "win"),
        P("clip", "win"),
        P("clip", "win"),
    )
    out_specs = (
        P("clip", "win", None),
        P("clip", "win", None),
        P("clip", "win"),
        P("clip", "win"),
        P("clip", "win"),
        P("clip", "win"),
        P("clip", "win"),
        P("clip", "win"),
        P("clip", "win"),
        P("win"),
        P(None, "win"),
        P("win", None),
        P("clip", None, "win"),
    )
    return jax.shard_map(local, mesh=mesh, in_specs=in_specs, out_specs=out_specs, check_vma=False)
```

```python
import functools
import math

import jax
import jax.numpy as jnp
from jax import lax
from jax.experimental import pallas as pl
from jax.experimental.pallas import tpu as pltpu
from jax.sharding import PartitionSpec as P

HEADS = 16
HD = 64
FRAMES = 5
GRID = 32
WS = 8
SEQ = 5120
WIN_TOK = 320
NREL = 2025
TXT = 77
QUAD = 4
QW = QUAD * HD
QUADS = HEADS // QUAD
SPAN = 2 * WS - 1
FSPAN = 2 * FRAMES - 1
SIDE = WS * WS
PAIR = 2 * HD
LANES = QUAD * WIN_TOK
TEXT_ROWS = 80
CHUNK = 256

epsilon = 1e-06
gelu_coefficient = 0.7978845608028654
scale_factor = HD ** (-0.5)
bfloat = jnp.bfloat16
single = jnp.float32
NEGATIVE = -1e30
VMEM_LIMIT = 60 * 1024 * 1024

NN = (((1,), (0,)), ((), ()))
NT = (((1,), (1,)), ((), ()))
TN = (((0,), (0,)), ((), ()))


def mm(left, right, dims=NN):
    return lax.dot_general(left, right, dims, preferred_element_type=single)


def norm_parts(values):
    centered = values - jnp.mean(values, axis=-1, keepdims=True)
    variance = jnp.mean(centered * centered, axis=-1, keepdims=True)
    inverse = lax.rsqrt(variance + epsilon)
    return centered * inverse, inverse


def norm_back(normed, inverse, grad):
    return inverse * (
        grad
        - jnp.mean(grad, axis=-1, keepdims=True)
        - normed * jnp.mean(grad * normed, axis=-1, keepdims=True)
    )


def params():
    return pltpu.CompilerParams(vmem_limit_bytes=VMEM_LIMIT)


def cost(microseconds):
    return pl.CostEstimate(
        flops=int(microseconds * 760e9),
        bytes_accessed=int(microseconds * 1e9),
        transcendentals=0,
    )


def tie(*values):
    return lax.optimization_barrier(values)


ANY = pl.BlockSpec(memory_space=pl.ANY)
PLACE = pl.BlockSpec(memory_space=pltpu.SMEM)
FIRST_ORDER = ("z", "x", "y")
OTHER_ORDER = ("z", "y", "x")


class Term:
    def __init__(self, kept, sent, lead):
        self.kept, self.sent, self.lead = kept, sent, lead


jax.tree_util.register_pytree_node(
    Term, lambda t: ((t.kept, t.sent), t.lead), lambda lead, parts: Term(*parts, lead)
)


class Layout:
    def __init__(self, clip_size, win_count):
        self.clip_size, self.win_count = clip_size, win_count
        y = 2 ** ((clip_size.bit_length() - 1) // 2)
        self.size = {"z": clip_size // y, "y": y, "x": win_count // 2, "core": 2}
        self.home = {"z": "clip", "y": "clip", "x": "win", "core": "win"}
        self.stride = {"z": y, "y": 1, "x": 2, "core": 1}
        self.others = clip_size * win_count // 2

    def place(self):
        clip, win = lax.axis_index("clip"), lax.axis_index("win")
        y = self.size["y"]
        return jnp.stack([clip // y, clip % y, win // 2, win % 2]).astype(jnp.int32)

    def swap(self, values, axis, apart):
        home = self.home[axis]
        count = self.clip_size if home == "clip" else self.win_count
        step = apart * self.stride[axis]
        return lax.ppermute(values, home, [(i, i ^ step) for i in range(count)])

    def gather(self, held, axis, apart, pin):
        part, pin = tie(self.swap(held, axis, apart), pin)
        return held, part, pin

    def gather_axis(self, held, axis, pin):
        apart = 1
        while apart < self.size[axis]:
            held, part, pin = self.gather(held, axis, apart, pin)
            held = jnp.concatenate([held, part], axis=0)
            apart *= 2
        return held, pin

    def gather_last(self, held, axis, pin):
        apart = 1
        while apart < self.size[axis] // 2:
            held, part, pin = self.gather(held, axis, apart, pin)
            held = jnp.concatenate([held, part], axis=0)
            apart *= 2
        return self.gather(held, axis, apart, pin)

    def with_other_core(self, *arrays):
        return list(arrays) + [self.swap(array, "core", 1) for array in arrays]

    def owner(self, place_ref, order, index, core_apart):
        names = ("z", "y", "x", "core")
        at = {name: place_ref[i] for i, name in enumerate(names)}
        for axis in order:
            at[axis] = at[axis] ^ (index % self.size[axis])
            index = index // self.size[axis]
        core = at["core"] ^ core_apart
        return at["z"] * self.size["y"] + at["y"], at["x"] * 2 + core

    def reduce(self, terms, axes, apart, pin):
        came = [self.swap(term.sent, axis, n) for term, axis, n in zip(terms, axes, apart)]
        came, pin = tie(came, pin)
        pairs = []
        for term, part in zip(terms, came):
            kept, lead = term.kept, term.lead
            while lead > 0 and kept.shape[0] == 1:
                kept, part, lead = kept[0], part[0], lead - 1
            pairs.append((kept, part))
        if lead == 0:
            sums = [kept.astype(single) + part.astype(single) for kept, part in pairs]
            return jnp.concatenate(sums, axis=0), pin
        return Term(*add_halves(pairs), lead), pin

    def reduce_axes(self, terms, axes, pin):
        terms = list(terms)
        for i, axis in enumerate(axes):
            for bit in range(self.bits(axis) - 1):
                terms[i], pin = self.reduce([terms[i]], [axis], [1 << bit], pin)
        return self.reduce(terms, axes, [self.size[axis] // 2 for axis in axes], pin)

    def bits(self, axis):
        return self.size[axis].bit_length() - 1


def add_kernel(*refs):
    ins, outs, at = refs[:-2], refs[-2:], 0
    for i in range(0, len(ins), 2):
        count = ins[i].shape[2]
        for half, out_ref in enumerate(outs):
            total = ins[i][half, 0].astype(single) + ins[i + 1][half, 0].astype(single)
            out_ref[0, at : at + count] = total.astype(bfloat)
        at += count


def add_halves(pairs):
    shape = pairs[0][0].shape
    lead = (shape[0] // 2,) + shape[1:-3]
    steps, total = math.prod(lead), sum(kept.shape[-3] for kept, _ in pairs)
    ins, in_specs = [], []
    for pair in pairs:
        tail = pair[0].shape[-3:]
        ins += [array.reshape((2, steps) + tail) for array in pair]
        in_specs += [pl.BlockSpec((2, 1) + tail, lambda i: (0, i, 0, 0, 0))] * 2
    tail = (total,) + shape[-2:]
    outs = pl.pallas_call(
        add_kernel,
        grid=(steps,),
        in_specs=in_specs,
        out_specs=[pl.BlockSpec((1,) + tail, lambda i: (i, 0, 0, 0))] * 2,
        out_shape=[jax.ShapeDtypeStruct((steps,) + tail, bfloat)] * 2,
        compiler_params=params(),
        cost_estimate=cost(0),
        name="add_halves",
    )(*ins)
    return [out.reshape(lead + tail) for out in outs]


def reverse(index, size):
    distance, bits = 0, size.bit_length() - 1
    for b in range(bits):
        distance = distance + (((index >> b) & 1) << (bits - 1 - b))
    return distance


def start_weight(sources, target, sem, layout, place_ref, order, cols, offset=0):
    half = len(sources) // 2
    for k, source in enumerate(sources):
        count, rows = source.shape[:2]

        def step(i, carry, source=source, k=k, count=count, rows=rows):
            clip, win = layout.owner(place_ref, order, i + k % half * count, k // half)
            row = pl.multiple_of(clip * rows, rows)
            column = pl.multiple_of(win * cols, cols)
            pltpu.make_async_copy(
                source.at[i, :, pl.ds(offset, cols)],
                target.at[pl.ds(row, rows), pl.ds(column, cols)],
                sem,
            ).start()
            return carry

        lax.fori_loop(0, count, step, 0)


def start_squares(sources, targets, sems, layout, place_ref):
    cols = sources[0].shape[2] // len(targets)
    for i, target in enumerate(targets):
        start_weight(sources, target, sems.at[i], layout, place_ref, FIRST_ORDER, cols, i * cols)


def start_gathered(source, target, sem, layout, cols, offset=0):
    depth = source.shape[1]
    rows = target.shape[0] // layout.clip_size

    def step(c, carry):
        for w in range(layout.win_count):
            for piece in range(rows // depth):
                row = pl.multiple_of(c * rows + piece * depth, depth)
                pltpu.make_async_copy(
                    source.at[c * layout.win_count + w, :, pl.ds(offset + piece * cols, cols)],
                    target.at[pl.ds(row, depth), pl.ds(w * cols, cols)],
                    sem,
                ).start()
        return carry

    lax.fori_loop(0, layout.clip_size, step, 0)


def wait_weight(target, sem):
    pltpu.make_async_copy(target, target, sem).wait()


def piece_spec(wins, width, frame):
    return pl.BlockSpec(
        (1, 1, WS, 1, WS, width), lambda i: (i // wins, frame, 0, i % wins, 0, 0)
    )


def whole_spec(wins, width):
    return pl.BlockSpec(
        (1, FRAMES, WS, 1, WS, width), lambda i: (i // wins, 0, 0, i % wins, 0, 0)
    )


def rows_spec(width):
    return pl.BlockSpec((1, WIN_TOK, width), lambda i: (i, 0, 0))


def modulation_spec(wins, width):
    return pl.BlockSpec((1, 6, width), lambda i: (i // wins, 0, 0))


def load_window(refs):
    parts = [ref[0, 0, :, 0].astype(single).reshape(SIDE, ref.shape[-1]) for ref in refs]
    return jnp.concatenate(parts, axis=0)


def store_window(refs, values):
    whole, others = refs[0], refs[1:]
    shape = (FRAMES, WS, WS, whole.shape[-1])
    values = values.reshape(shape).astype(whole.dtype)
    if not others:
        whole[0, :, :, 0] = values
        return
    whole[0, 0, :, 0] = values[0]
    whole[0, FRAMES - 1, :, 0] = values[1]
    for i, other in enumerate(others):
        other[0, 0, :, 0] = values[2 + i]


def store_units(ref, index, first, values):
    unit = ref.shape[-1]
    for at in range(0, values.shape[1], unit):
        ref[index, (first + at) // unit, 0] = values[:, at : at + unit]


def frame_offset(shift, query, key):
    return lax.rem(shift + query, FRAMES) - lax.rem(shift + key, FRAMES) + FRAMES - 1


def frame_blocks():
    for key in range(FRAMES):
        for query in range(FRAMES):
            for pair in range(QUAD // 2):
                lane = query * QW + pair * PAIR
                yield key, query, pair, slice(key * SIDE, (key + 1) * SIDE), slice(lane, lane + PAIR)


def table_kernel(shift_ref, block_ref, out_ref):
    for key, query, pair, rows, lanes in frame_blocks():
        offset = frame_offset(shift_ref[0], query, key)
        out_ref[0, rows, lanes] = block_ref[pair, offset]


def collect_kernel(shift_ref, sum_ref, out_ref, pairs_ref):
    pairs_ref[...] = jnp.zeros(pairs_ref.shape, single)
    for key, query, pair, rows, lanes in frame_blocks():
        offset = frame_offset(shift_ref[0], query, key)
        pairs_ref[pair, offset] += sum_ref[0, rows, lanes]
    for head in range(QUAD):
        lanes = slice(head % 2 * HD, (head % 2 + 1) * HD)
        out_ref[head] = pairs_ref[head // 2, :, :, lanes]


QUAD_SPEC = pl.BlockSpec((1, WIN_TOK, LANES), lambda q, s: (q, 0, 0))
BLOCKS_SPEC = pl.BlockSpec((QUAD // 2, FSPAN, SIDE, PAIR), lambda q, s: (q, 0, 0, 0))


def side_hot():
    shape = (SPAN * SPAN, SIDE * SIDE)
    offset = lax.broadcasted_iota(jnp.int32, shape, 0)
    pair = lax.broadcasted_iota(jnp.int32, shape, 1)
    key, query = pair // SIDE, pair % SIDE
    rows = query // WS - key // WS + WS - 1
    columns = query % WS - key % WS + WS - 1
    return (rows * SPAN + columns == offset).astype(single)


def table_blocks(bias_full):
    flat = bias_full.reshape(HEADS * FSPAN, SPAN * SPAN)
    blocks = jnp.dot(flat, side_hot(), precision=lax.Precision.HIGHEST)
    blocks = blocks.reshape(HEADS // 2, 2, FSPAN, SIDE, SIDE).transpose(0, 2, 3, 1, 4)
    return blocks.reshape(HEADS // 2, FSPAN, SIDE, PAIR)


def bias_table(blocks, shift):
    return pl.pallas_call(
        table_kernel,
        grid_spec=pltpu.PrefetchScalarGridSpec(
            num_scalar_prefetch=1,
            grid=(QUADS,),
            in_specs=[BLOCKS_SPEC],
            out_specs=QUAD_SPEC,
        ),
        out_shape=jax.ShapeDtypeStruct((QUADS, WIN_TOK, LANES), single),
        compiler_params=params(),
        cost_estimate=cost(5),
        name="bias_table",
    )(shift, blocks)


def bias_blocks(bias_sum, shift):
    return pl.pallas_call(
        collect_kernel,
        grid_spec=pltpu.PrefetchScalarGridSpec(
            num_scalar_prefetch=1,
            grid=(QUADS,),
            in_specs=[QUAD_SPEC],
            out_specs=pl.BlockSpec((QUAD, FSPAN, SIDE, SIDE), lambda q, s: (q, 0, 0, 0)),
            scratch_shapes=[pltpu.VMEM((QUAD // 2, FSPAN, SIDE, PAIR), single)],
        ),
        out_shape=jax.ShapeDtypeStruct((HEADS, FSPAN, SIDE, SIDE), single),
        compiler_params=params(),
        cost_estimate=cost(5),
        name="bias_collect",
    )(shift, bias_sum).reshape(HEADS * FSPAN, SIDE * SIDE)


def bias_collect(flat):
    summed = lax.dot_general(flat, side_hot(), NT, precision=lax.Precision.HIGHEST)
    return summed.reshape(HEADS, NREL)


def project_kernel(layout, *refs):
    token_refs, refs = refs[:FRAMES], refs[FRAMES:]
    mod_ref, weight_any, low_ref, out_ref, weight_ref, sem = refs

    @pl.when(pl.program_id(0) == 0)
    def _():
        start_gathered(weight_any, weight_ref, sem, layout, weight_any.shape[2])
        wait_weight(weight_ref, sem)

    normed, _ = norm_parts(load_window(token_refs))
    low = (normed * (1.0 + mod_ref[0, 1:2]) + mod_ref[0, 0:1]).astype(bfloat)
    low_ref[0] = low
    out_ref[0] = mm(low, weight_ref[...]).astype(bfloat)


def head_mask(rows, head):
    lane = lax.broadcasted_iota(jnp.int32, (rows, QW), 1)
    return (lane >= head * HD) & (lane < (head + 1) * HD)


def spread(values):
    masks = [head_mask(SIDE, h) for h in range(QUAD)]
    parts = []
    for frame in range(FRAMES):
        rows = values[frame * SIDE : (frame + 1) * SIDE]
        parts += [jnp.where(mask, rows, jnp.zeros_like(rows)) for mask in masks]
    return jnp.concatenate(parts, axis=0)


def own_heads(product):
    lane = lax.broadcasted_iota(jnp.int32, (SIDE, PAIR), 1)
    rows = []
    for frame in range(FRAMES):
        parts = []
        for pair in range(QUAD // 2):
            at = frame * QW + pair * PAIR
            block = product[pair * PAIR : (pair + 1) * PAIR, at : at + PAIR].T
            parts.append(jnp.where(lane < HD, block[:SIDE], block[SIDE:]))
        rows.append(jnp.concatenate(parts, axis=1))
    return jnp.concatenate(rows, axis=0)


def softmax_down(scores):
    expanded = jnp.exp(scores - jnp.max(scores, axis=0, keepdims=True))
    return expanded * (1.0 / jnp.sum(expanded, axis=0, keepdims=True))


def lane_chunks():
    return [slice(c, c + CHUNK) for c in range(0, LANES, CHUNK)]


def attend_kernel(projected_ref, bias_ref, out_ref, probs_ref, scores_ref):
    width = out_ref.shape[-1]
    for q in range(QUADS):
        at, slot = slice(q * QW, (q + 1) * QW), q % 2
        queries = spread(projected_ref[0, :, at] * jnp.asarray(scale_factor, bfloat))
        keys = projected_ref[0, :, width + q * QW : width + (q + 1) * QW]
        values = projected_ref[0, :, 2 * width + q * QW : 2 * width + (q + 1) * QW]
        scores_ref[slot] = mm(keys, queries, NT)
        for lanes in lane_chunks():
            scores = scores_ref[slot, :, lanes] + bias_ref[q, :, lanes]
            probs_ref[0, q, :, lanes] = softmax_down(scores).astype(bfloat)
        out_ref[0, :, at] = own_heads(mm(values, probs_ref[0, q], TN)).astype(bfloat)


def attend_back_kernel(
    projected_ref, grad_ref, probs_ref, out_ref, sum_ref, grad_probs_ref, grad_scores_ref
):
    @pl.when(pl.program_id(0) == 0)
    def _():
        sum_ref[...] = jnp.zeros(sum_ref.shape, single)

    width = grad_ref.shape[-1]
    for q in range(QUADS):
        at, slot = slice(q * QW, (q + 1) * QW), q % 2
        queries = spread(projected_ref[0, :, at] * jnp.asarray(scale_factor, bfloat))
        keys = projected_ref[0, :, width + q * QW : width + (q + 1) * QW]
        values = projected_ref[0, :, 2 * width + q * QW : 2 * width + (q + 1) * QW]
        grads = spread(grad_ref[0, :, at])
        grad_probs_ref[slot] = mm(values, grads, NT)
        store_units(out_ref, 2, q * QW, mm(probs_ref[0, q], grads).astype(bfloat))
        for lanes in lane_chunks():
            probs = probs_ref[0, q, :, lanes].astype(single)
            weighted = probs * grad_probs_ref[slot, :, lanes]
            grad_scores = weighted - probs * jnp.sum(weighted, axis=0, keepdims=True)
            grad_scores_ref[slot, :, lanes] = grad_scores.astype(bfloat)
            sum_ref[q, :, lanes] += grad_scores
        store_units(out_ref, 1, q * QW, mm(grad_scores_ref[slot], queries).astype(bfloat))
        grad_queries = own_heads(mm(keys, grad_scores_ref[slot], TN))
        store_units(out_ref, 0, q * QW, (grad_queries * scale_factor).astype(bfloat))


BIAS_SPEC = pl.BlockSpec((QUADS, WIN_TOK, LANES), lambda i: (0, 0, 0))
PROBS_SPEC = pl.BlockSpec((1, QUADS, WIN_TOK, LANES), lambda i: (i, 0, 0, 0))


def memory_kernel(layout, place_ref, text_ref, *refs):
    sources, (memory_ref, weight_ref, sem) = refs[:4], refs[4:]

    @pl.when(pl.program_id(0) == 0)
    def _():
        cols = sources[0].shape[2]
        start_weight(sources, weight_ref, sem, layout, place_ref, OTHER_ORDER, cols)
        wait_weight(weight_ref, sem)

    memory_ref[0] = mm(text_ref[0], weight_ref[...]).astype(bfloat)


def cross_probs(queries, keys):
    scores = mm(keys, queries, NT)
    whole = TXT // 8 * 8
    row = lax.broadcasted_iota(jnp.int32, (TEXT_ROWS - whole, LANES), 0) + whole
    rest = jnp.where(row < TXT, scores[whole:], NEGATIVE)
    return softmax_down(jnp.concatenate([scores[:whole], rest], axis=0))


def cross_kernel(layout, place_ref, *refs):
    token_refs, refs = refs[:FRAMES], refs[FRAMES:]
    attended_ref, mod_ref, gain_ref, memory_ref = refs[:4]
    sources, refs = refs[4:8], refs[8:]
    branch_ref, left_ref, queries_ref, sum_ref, output_ref, query_ref, cross_ref, sems = refs

    @pl.when(pl.program_id(0) == 0)
    def _():
        start_squares(sources, (output_ref, query_ref, cross_ref), sems, layout, place_ref)
        wait_weight(output_ref, sems.at[0])
        wait_weight(query_ref, sems.at[1])
        wait_weight(cross_ref, sems.at[2])

    attended = attended_ref[0]
    left_ref[0, 0] = attended
    branch = mm(attended, output_ref[...])
    branch_ref[0] = branch
    first_sum = load_window(token_refs) + mod_ref[0, 2:3] * branch
    normed, _ = norm_parts(first_sum)
    second = (normed * gain_ref[...]).astype(bfloat)
    left_ref[1, 0] = second
    queries = mm(second, query_ref[...]).astype(bfloat)
    queries_ref[0] = queries
    width = queries.shape[1]
    parts = []
    for q in range(QUADS):
        at = slice(q * QW, (q + 1) * QW)
        scaled = spread(queries[:, at] * jnp.asarray(scale_factor, bfloat))
        probs = cross_probs(scaled, memory_ref[0, :, at]).astype(bfloat)
        values = memory_ref[0, :, width + q * QW : width + (q + 1) * QW]
        parts.append(own_heads(mm(values, probs, TN)).astype(bfloat))
    crossed = jnp.concatenate(parts, axis=1)
    left_ref[2, 0] = crossed
    sum_ref[0] = first_sum + mm(crossed, cross_ref[...])


def cross_back_kernel(layout, wins, place_ref, *refs):
    token_refs, refs = refs[:FRAMES], refs[FRAMES:]
    mod_ref, gain_ref, memory_ref, grad_ref, queries_ref, branch_ref = refs[:6]
    sources, refs = refs[6:10], refs[10:]
    right_ref, grad_sum_ref, grad_attended_ref = refs[:3]
    grad_memory_ref, gain_grad_ref, gate_grad_ref = refs[3:6]
    output_ref, query_ref, cross_ref, sems = refs[6:]
    step = pl.program_id(0)

    @pl.when(step == 0)
    def _():
        start_squares(sources, (output_ref, query_ref, cross_ref), sems, layout, place_ref)
        wait_weight(output_ref, sems.at[0])
        wait_weight(query_ref, sems.at[1])
        wait_weight(cross_ref, sems.at[2])
        gain_grad_ref[...] = jnp.zeros(gain_grad_ref.shape, single)

    @pl.when(step % wins == 0)
    def _():
        grad_memory_ref[...] = jnp.zeros(grad_memory_ref.shape, single)
        gate_grad_ref[...] = jnp.zeros(gate_grad_ref.shape, single)

    width = queries_ref.shape[-1]
    grad = grad_ref[0]
    grad_low = grad.astype(bfloat)
    store_units(right_ref, 2, 0, grad_low)
    grad_crossed = mm(grad_low, cross_ref[...], NT).astype(bfloat)
    queries = queries_ref[0]
    query_parts = []
    for q in range(QUADS):
        at = slice(q * QW, (q + 1) * QW)
        value_at = slice(width + q * QW, width + (q + 1) * QW)
        scaled = spread(queries[:, at] * jnp.asarray(scale_factor, bfloat))
        grads = spread(grad_crossed[:, at])
        keys = memory_ref[0, :, at]
        probs = cross_probs(scaled, keys)
        weighted = probs * mm(memory_ref[0, :, value_at], grads, NT)
        grad_scores = weighted - probs * jnp.sum(weighted, axis=0, keepdims=True)
        grad_scores = grad_scores.astype(bfloat)
        grad_memory_ref[0, :, at] += mm(grad_scores, scaled)
        grad_memory_ref[0, :, value_at] += mm(probs.astype(bfloat), grads)
        part = own_heads(mm(keys, grad_scores, TN))
        query_parts.append((part * scale_factor).astype(bfloat))
    grad_queries = jnp.concatenate(query_parts, axis=1)
    store_units(right_ref, 1, 0, grad_queries)
    grad_second = mm(grad_queries, query_ref[...], NT)
    branch = branch_ref[0]
    normed, inverse = norm_parts(load_window(token_refs) + mod_ref[0, 2:3] * branch)
    gain_grad_ref[...] += jnp.sum(grad_second * normed, axis=0, keepdims=True)
    grad_sum = grad + norm_back(normed, inverse, grad_second * gain_ref[...])
    grad_sum_ref[0] = grad_sum
    gate_grad_ref[0] += jnp.sum(grad_sum * branch, axis=0, keepdims=True)
    grad_branch = (mod_ref[0, 2:3] * grad_sum).astype(bfloat)
    store_units(right_ref, 0, 0, grad_branch)
    grad_attended_ref[0] = mm(grad_branch, output_ref[...], NT).astype(bfloat)


def null_kernel(layout, place_ref, masked_ref, *refs):
    sources, (out_ref, weight_ref, sem) = refs[:4], refs[4:]
    cols = sources[0].shape[2]
    start_weight(sources, weight_ref, sem, layout, place_ref, OTHER_ORDER, cols)
    wait_weight(weight_ref, sem)
    masked = masked_ref[...]
    high = masked.astype(bfloat)
    rest = (masked - high.astype(single)).astype(bfloat)
    weight = weight_ref[...]
    out_ref[...] = mm(high, weight, NT) + mm(rest, weight, NT)


def null_text_term(layout, place, masked, sources):
    width = masked.shape[1] // 2
    whole = pl.BlockSpec(memory_space=pltpu.VMEM)
    return pl.pallas_call(
        functools.partial(null_kernel, layout),
        in_specs=[PLACE, whole, ANY, ANY, ANY, ANY],
        out_specs=whole,
        out_shape=jax.ShapeDtypeStruct((masked.shape[0], width), single),
        scratch_shapes=[pltpu.VMEM((width, 2 * width), bfloat), pltpu.SemaphoreType.DMA(())],
        compiler_params=params(),
        cost_estimate=cost(5),
        name="null_text",
    )(place, masked, *sources)


def feed_kernel(layout, wins, chunk, sent, *refs):
    grad_out_refs, refs = refs[:FRAMES], refs[FRAMES:]
    sum_ref, mod_ref, weights_any = refs[:3]
    out_refs, refs = refs[3 : 4 + sent], refs[4 + sent :]
    third_ref, act_ref, grad_hidden_ref, grad_reduced_ref, grad_sum_ref, grad_mod_ref = refs[:6]
    expand_ref, reduce_ref, sems = refs[6:]
    step = pl.program_id(0)

    @pl.when(step == 0)
    def _():
        cols = expand_ref.shape[1] // layout.win_count
        start_gathered(weights_any, expand_ref, sems.at[0], layout, cols)
        offset = cols
        cols = reduce_ref.shape[1] // layout.win_count
        start_gathered(weights_any, reduce_ref, sems.at[1], layout, cols, offset)
        wait_weight(expand_ref, sems.at[0])
        wait_weight(reduce_ref, sems.at[1])

    @pl.when(step % wins == 0)
    def _():
        grad_mod_ref[...] = jnp.zeros(grad_mod_ref.shape, single)

    second_sum = sum_ref[0]
    normed, inverse = norm_parts(second_sum)
    third = (normed * (1.0 + mod_ref[0, 4:5]) + mod_ref[0, 3:4]).astype(bfloat)
    third_ref[0] = third
    grad_out = load_window(grad_out_refs)
    gate = mod_ref[0, 5:6]
    grad_reduced = (gate * grad_out).astype(bfloat)
    grad_reduced_ref[0] = grad_reduced
    hidden_width = expand_ref.shape[1]
    for at in range(0, hidden_width, chunk):
        part = slice(at, at + chunk)
        v = mm(third, expand_ref[:, part])
        grad_act = mm(grad_reduced, reduce_ref[part], NT)
        square = v * v
        tanh = jnp.tanh(gelu_coefficient * (v + 0.044715 * (square * v)))
        half = 0.5 * (1.0 + tanh)
        act_ref[0, :, part] = (v * half).astype(bfloat)
        slope = half + (0.5 * gelu_coefficient) * v * (1.0 - tanh * tanh) * (
            1.0 + (3 * 0.044715) * square
        )
        grad_hidden_ref[0, :, part] = (grad_act * slope).astype(bfloat)
    reduced = mm(act_ref[0], reduce_ref[...])
    store_window(out_refs, second_sum + gate * reduced)
    grad_third = mm(grad_hidden_ref[0], expand_ref[...], NT)
    grad_mod_ref[0, 0:1] += jnp.sum(grad_third, axis=0, keepdims=True)
    grad_mod_ref[0, 1:2] += jnp.sum(grad_third * normed, axis=0, keepdims=True)
    grad_mod_ref[0, 2:3] += jnp.sum(grad_out * reduced, axis=0, keepdims=True)
    grad_sum_ref[0] = grad_out + norm_back(normed, inverse, grad_third * (1.0 + mod_ref[0, 4:5]))


def input_back_kernel(layout, wins, sent, *refs):
    token_refs, refs = refs[:FRAMES], refs[FRAMES:]
    mod_ref, grad_ref, grad_sum_ref, weight_any = refs[:4]
    out_refs, (grad_mod_ref, weight_ref, sem) = refs[4 : 5 + sent], refs[5 + sent :]
    step = pl.program_id(0)

    @pl.when(step == 0)
    def _():
        start_gathered(weight_any, weight_ref, sem, layout, weight_any.shape[2])
        wait_weight(weight_ref, sem)

    @pl.when(step % wins == 0)
    def _():
        grad_mod_ref[...] = jnp.zeros(grad_mod_ref.shape, single)

    units = [grad_ref[k, u, 0] for k in range(3) for u in range(grad_ref.shape[1])]
    grads = jnp.concatenate(units, axis=1)
    grad_first = mm(grads, weight_ref[...], NT)
    normed, inverse = norm_parts(load_window(token_refs))
    grad_mod_ref[0, 0:1] += jnp.sum(grad_first, axis=0, keepdims=True)
    grad_mod_ref[0, 1:2] += jnp.sum(grad_first * normed, axis=0, keepdims=True)
    back = norm_back(normed, inverse, grad_first * (1.0 + mod_ref[0, 1:2]))
    store_window(out_refs, grad_sum_ref[0] + back)


def owner_column(layout, place_ref, step, core_apart):
    distance = reverse(step, layout.size["x"])
    return (place_ref[2] ^ distance) * 2 + (place_ref[3] ^ core_apart)


def owner_row(layout, place_ref, y, z):
    y, z = reverse(y, layout.size["y"]), reverse(z, layout.size["z"])
    return (place_ref[0] ^ z) * layout.size["y"] + (place_ref[1] ^ y)


def columns_kernel(layout, pieces, added, x_first, pair, place_ref, x_ref, *refs):
    outs = 2 if pair else 1
    y_refs, out_refs, product_ref = refs[:pieces], refs[-1 - outs : -1], refs[-1]
    split, rows, width = out_refs[0].shape[-3:]
    cols = product_ref.shape[1] // pieces
    for i in range(pieces):
        product_ref[:, i * cols : (i + 1) * cols] = mm(x_ref[0], y_refs[i][0], TN)

    def store(out_ref, first_y, last_y):
        for y in range(first_y, last_y):
            for z in range(layout.size["z"]):
                clip = owner_row(layout, place_ref, y, z)
                part = product_ref[pl.ds(pl.multiple_of(clip * rows, rows), rows)]
                for i in range(split):
                    piece = part[:, i * width : (i + 1) * width]
                    if added:
                        at = (0, y, z, i) if x_first else (y, 0, z, i)
                        piece = piece + refs[pieces][at].astype(single)
                    at = (0, y, z, i) if x_first else (y - first_y, 0, z, i)
                    out_ref[at] = piece.astype(bfloat)

    size_y = layout.size["y"]
    if not pair:
        store(out_refs[0], 0, size_y)
    elif x_first:
        half = layout.size["x"] // 2
        pl.when(pl.program_id(1) < half)(lambda: store(out_refs[0], 0, size_y))
        pl.when(pl.program_id(1) >= half)(lambda: store(out_refs[1], 0, size_y))
    else:
        store(out_refs[0], 0, size_y // 2)
        store(out_refs[1], size_y // 2, size_y)


def weight_grad(
    layout, place, x, y, pieces, added, name, x_first=False, split=1, entries=None, into=None, first=0
):
    pair = added is not None
    core_apart = 0 if pair else 1
    count, tokens, depth = x.shape
    unit = y.shape[-1] if y.ndim == 4 else y.shape[-1] // layout.win_count
    rows, cols = depth // layout.clip_size, pieces * unit
    size = layout.size

    def unit_spec(i):
        def index(n, j, place_ref):
            at = owner_column(layout, place_ref, j, core_apart) * pieces + i
            return (n * pieces + at // layout.win_count, 0, at % layout.win_count)

        if y.ndim == 3:
            return pl.BlockSpec((1, tokens, unit), index)

        def unit_index(n, j, place_ref):
            entry, _, at = index(n, j, place_ref)
            return (entry, at, 0, 0)

        return pl.BlockSpec((1, None, tokens, unit), unit_index)

    axes = ("x", "y", "z") if x_first else ("y", "x", "z")
    leading = tuple(size[axis] for axis in axes)
    half = leading[0] // 2

    def block(start, part):
        step = size["x"] if part is None else half
        lead = (1,) + leading[1:] if x_first else (leading[0] if part is None else half, 1, size["z"])

        def index(n, j, place_ref):
            at = n + start // split
            if not x_first:
                return (0, j, 0, at, 0, 0)
            if part is not None:
                j = jnp.clip(j - part * half, 0, step - 1)
            return (j, 0, 0, at, 0, 0)

        return pl.BlockSpec(lead + (split, rows, cols // split), index)

    if pair:
        out_specs = [block(first, 0), block(first, 1)]
        total = entries or count * split
        out_lead = (half,) + leading[1:]
    else:
        out_specs = [block(0, None)]
        total, out_lead = count * split, leading
    extra = ([added] if pair else []) + ([into.kept, into.sent] if into else [])
    extra_specs = ([block(0, None)] if pair else []) + ([ANY, ANY] if into else [])
    start = 2 + pieces + (1 if pair else 0)
    out_shape = jax.ShapeDtypeStruct(out_lead + (total, rows, cols // split), bfloat)
    outs = pl.pallas_call(
        functools.partial(columns_kernel, layout, pieces, pair, x_first, pair),
        grid_spec=pltpu.PrefetchScalarGridSpec(
            num_scalar_prefetch=1,
            grid=(count, size["x"]),
            in_specs=[pl.BlockSpec((1, tokens, depth), lambda n, j, p: (n, 0, 0))]
            + [unit_spec(i) for i in range(pieces)]
            + extra_specs,
            out_specs=out_specs,
            scratch_shapes=[pltpu.VMEM((depth, cols), single)],
        ),
        out_shape=[out_shape] * len(out_specs),
        input_output_aliases={start: 0, start + 1: 1} if into else {},
        compiler_params=params(),
        cost_estimate=cost(count * size["x"] * tokens * depth * cols / 382e3),
        name=name,
    )(place, x, *([y] * pieces), *extra)
    return Term(outs[0], outs[1], 3) if pair else outs[0]


def rows_kernel(layout, pair, place_ref, x_ref, *refs):
    size = layout.size["x"]
    y_refs, out_refs = refs[:size], refs[-2 if pair else -1 :]
    left = x_ref[...]

    def store(out_ref):
        for j in range(size):
            part = mm(left, y_refs[j][...], TN).reshape(out_ref.shape[3:])
            if pair:
                part = part + refs[size][0, j, 0].astype(single)
            out_ref[0, j, 0] = part.astype(bfloat)

    if not pair:
        store(out_refs[0])
        return
    half = layout.size["y"] // 2
    pl.when(pl.program_id(0) < half)(lambda: store(out_refs[0]))
    pl.when(pl.program_id(0) >= half)(lambda: store(out_refs[1]))


def weight_grad_rows(layout, place, x, y, split, added, name):
    tokens, depth = x.shape
    width = y.shape[1]
    rows, cols = depth // layout.clip_size, width // layout.win_count
    size = layout.size
    half = size["y"] // 2
    pair = added is not None

    def left(y_at, z_at, place_ref):
        return (0, owner_row(layout, place_ref, y_at, z_at))

    def right(j):
        return lambda y_at, z_at, place_ref: (
            0,
            owner_column(layout, place_ref, j, 0 if pair else 1),
        )

    def block(part):
        def index(y_at, z_at, place_ref):
            if part == 0:
                z_at = jnp.where(y_at < half, z_at, size["z"] - 1)
                y_at = jnp.minimum(y_at, half - 1)
            elif part == 1:
                z_at = jnp.where(y_at < half, 0, z_at)
                y_at = jnp.maximum(y_at - half, 0)
            return (y_at, 0, z_at, 0, 0, 0)

        return pl.BlockSpec((1, size["x"], 1, split, rows // split, cols), index)

    out_lead = (half if pair else size["y"], size["x"], size["z"])
    out_shape = jax.ShapeDtypeStruct(out_lead + (split, rows // split, cols), bfloat)
    outs = pl.pallas_call(
        functools.partial(rows_kernel, layout, pair),
        grid_spec=pltpu.PrefetchScalarGridSpec(
            num_scalar_prefetch=1,
            grid=(size["y"], size["z"]),
            in_specs=[pl.BlockSpec((tokens, rows), left)]
            + [pl.BlockSpec((tokens, cols), right(j)) for j in range(size["x"])]
            + [block(None)] * pair,
            out_specs=[block(0), block(1)] if pair else [block(None)],
        ),
        out_shape=[out_shape] * (2 if pair else 1),
        compiler_params=params(),
        cost_estimate=cost(size["x"] * tokens * depth * cols / 382e3),
        name=name,
    )(place, x, *([y] * size["x"]), *([added] if pair else []))
    return Term(outs[0], outs[1], 3) if pair else outs[0]


def to_windows(values, win_count):
    clips, count, width = values.shape
    blocks = GRID // WS
    if win_count == blocks:
        own = values.reshape(clips, FRAMES, WS, blocks, WS, width)
        received = []
        for k in range(blocks - 1, 0, -1):
            pairs = [(w, (w + k) % win_count) for w in range(win_count)]
            received.append((lax.ppermute(own[:, k : k + 1], "win", pairs), 0))
        return [(own, 0), (own, FRAMES - 1)] + received
    halves = win_count // blocks
    wins = blocks // halves
    me = lax.axis_index("win")
    whole = lax.all_gather(values, "win", axis=1, tiled=True)
    whole = whole.reshape(clips, FRAMES, blocks, WS, blocks, WS, width)
    whole = lax.dynamic_slice_in_dim(whole, me // halves, 1, axis=2)
    whole = lax.dynamic_slice_in_dim(whole, (me % halves) * wins, wins, axis=4)
    whole = whole.reshape(clips, FRAMES, WS, wins, WS, width)
    return [(whole, f) for f in range(FRAMES)]


def sent_count(win_count):
    return FRAMES - 2 if win_count == GRID // WS else 0


def send_back(sent, win_count, pin):
    blocks = GRID // WS
    received = []
    for i, array in enumerate(sent):
        k = blocks - 1 - i
        pairs = [((w + k) % win_count, w) for w in range(win_count)]
        received.append(lax.ppermute(array, "win", pairs))
    return tie(received, pin)


def put_together(whole, received, win_count):
    clips, _, _, wins, _, width = whole.shape
    blocks = GRID // WS
    if win_count == blocks:
        for i, array in enumerate(received):
            whole = lax.dynamic_update_slice_in_dim(whole, array, blocks - 1 - i, axis=1)
        return whole.reshape(clips, FRAMES * WS * blocks * WS, width)
    halves = win_count // blocks
    me = lax.axis_index("win")
    whole = lax.all_gather(whole, "win", axis=0, tiled=False)
    whole = whole.reshape(blocks, halves, clips, FRAMES, WS, wins, WS, width)
    whole = whole.transpose(2, 3, 0, 4, 1, 5, 6, 7).reshape(clips, SEQ, width)
    count = SEQ // win_count
    return lax.dynamic_slice_in_dim(whole, me * count, count, axis=1)


def gather_first(arrays, squares, layout):
    me = lax.axis_index("win")
    held, squares = jnp.concatenate([a.reshape(-1) for a in arrays])[None], squares[None]
    win_bits = layout.win_count.bit_length() - 1
    for bit in range(max(win_bits, layout.bits("z"))):
        apart, came, part = layout.win_count >> (bit + 1), held, squares
        if bit < win_bits:
            pairs = [(i, i ^ apart) for i in range(layout.win_count)]
            came = lax.ppermute(held, "win", pairs)
        if bit < layout.bits("z"):
            part = layout.swap(squares, "z", 1 << bit)
        came, part = tie(came, part)
        if bit < win_bits:
            upper = (me & apart) > 0
            first, second = jnp.where(upper, came, held), jnp.where(upper, held, came)
            held = jnp.stack([first, second], axis=1).reshape(2 * held.shape[0], held.shape[1])
        if bit < layout.bits("z"):
            squares = jnp.concatenate([squares, part], axis=0)
    outs, at = [], 0
    for a in arrays:
        outs.append(held[:, at : at + a.size].reshape((layout.win_count,) + a.shape))
        at += a.size
    return outs, squares


def sum_over_win(values, layout):
    me = lax.axis_index("win")
    apart = layout.win_count // 2
    while apart > 0:
        upper = (me & apart) > 0
        first, second = values[:apart], values[apart:]
        sent = jnp.where(upper, first, second)
        kept = jnp.where(upper, second, first)
        pairs = [(i, i ^ apart) for i in range(layout.win_count)]
        values = kept + lax.ppermute(sent, "win", pairs)
        apart //= 2
    return values[0]


def sum_over_clip(values, layout, apart, end):
    while apart < end:
        pairs = [(i, i ^ apart) for i in range(layout.clip_size)]
        values = values + lax.ppermute(values, "clip", pairs)
        apart *= 2
    return values


def local(
    tokens,
    cotangent,
    modulation,
    text_features,
    null_mask,
    null_text,
    norm_gain,
    position_bias,
    self_input,
    self_output,
    cross_query,
    cross_memory,
    cross_output,
    expand_weight,
    reduce_weight,
):
    win_count = lax.axis_size("win")
    clip_size = lax.axis_size("clip")
    layout = Layout(clip_size, win_count)
    place = layout.place()
    blocks = GRID // WS
    clips, _, width = tokens.shape
    hidden_width = reduce_weight.shape[0] * clip_size
    both = ("clip", "win")
    me = lax.axis_index("win")

    input_all = lax.all_gather(self_input, both, axis=0, tiled=False)
    small = [position_bias, norm_gain.astype(single), null_text.astype(single)]
    squares = jnp.concatenate([self_output, cross_query, cross_output, cross_memory], axis=1)
    (bias_full, gain_full, null_full), squares = gather_first(small, squares, layout)
    bias_full = bias_full.reshape(HEADS, NREL)
    pieces = to_windows(tokens, win_count)
    wins = pieces[0][0].shape[3]
    windows = clips * wins
    count = windows * WIN_TOK
    sent = sent_count(win_count)
    columns = width // win_count
    gain_full = gain_full.reshape(1, width)
    null_full = null_full.transpose(1, 0, 2).reshape(TXT, width).astype(bfloat)
    shift = me if win_count == blocks else jnp.int32(0)
    shift = jnp.asarray(shift, jnp.int32).reshape(1)
    blocks_of_bias = table_blocks(bias_full)
    memory_part, squares_part = squares[:, :, 3 * columns :], squares[:, :, : 3 * columns]
    memory_part, blocks_of_bias = layout.gather_axis(memory_part, "y", blocks_of_bias)
    squares_part, blocks_of_bias = layout.gather_axis(squares_part, "x", blocks_of_bias)
    memory_part, squares_part, blocks_of_bias = tie(memory_part, squares_part, blocks_of_bias)
    table = bias_table(blocks_of_bias, shift)
    table, arrays = tie(table, [p[0] for p in pieces])
    pieces = [(array, frame) for array, (_, frame) in zip(arrays, pieces)]
    depth = expand_weight.shape[0]
    feed_shard = jnp.concatenate(
        [expand_weight]
        + [reduce_weight[i : i + depth] for i in range(0, reduce_weight.shape[0], depth)],
        axis=1,
    )
    feed_all = lax.all_gather(feed_shard, both, axis=0, tiled=False)

    token_specs = [piece_spec(wins, width, frame) for _, frame in pieces]
    tokens_in = [array for array, _ in pieces]

    shape = jax.ShapeDtypeStruct
    rows = functools.partial(shape, dtype=bfloat)
    wide = rows((windows, WIN_TOK, width))
    triple = rows((3, windows, WIN_TOK, width))
    triple_spec = pl.BlockSpec((3, 1, WIN_TOK, width), lambda i: (0, i, 0, 0))
    units = rows((3, win_count, windows, WIN_TOK, columns))
    units_spec = pl.BlockSpec((3, win_count, 1, WIN_TOK, columns), lambda i: (0, 0, i, 0, 0))
    wide_single = shape((windows, WIN_TOK, width), single)
    DMA = pltpu.SemaphoreType.DMA

    first_low, projected = pl.pallas_call(
        functools.partial(project_kernel, layout),
        grid=(windows,),
        in_specs=token_specs + [modulation_spec(wins, width), ANY],
        out_specs=[rows_spec(width), rows_spec(3 * width)],
        out_shape=[wide, rows((windows, WIN_TOK, 3 * width))],
        scratch_shapes=[pltpu.VMEM((width, 3 * width), bfloat), DMA(())],
        compiler_params=params(),
        cost_estimate=cost(26),
        name="project",
    )(*tokens_in, modulation, input_all)
    memory_near, memory_far, projected = layout.gather_last(memory_part, "x", projected)
    squares_near, squares_far, projected = layout.gather_last(squares_part, "y", projected)
    memory_all = layout.with_other_core(memory_near, memory_far)
    squares_all = layout.with_other_core(squares_near, squares_far)

    attended, probs = pl.pallas_call(
        attend_kernel,
        grid=(windows,),
        in_specs=[rows_spec(3 * width), BIAS_SPEC],
        out_specs=[rows_spec(width), PROBS_SPEC],
        out_shape=[wide, rows((windows, QUADS, WIN_TOK, LANES))],
        scratch_shapes=[pltpu.VMEM((2, WIN_TOK, LANES), single)],
        compiler_params=params(),
        cost_estimate=cost(37),
        name="attend",
    )(projected, table)

    cotangent, attended = tie(cotangent, attended)
    grad_pieces = to_windows(cotangent, win_count)

    null_flags = null_mask > 0
    used_text = jnp.where(null_flags[:, None, None], null_full[None], text_features)
    text_padded = jnp.pad(used_text, ((0, 0), (0, TEXT_ROWS - TXT), (0, 0)))
    text_spec = pl.BlockSpec((1, TEXT_ROWS, width), lambda i: (i, 0, 0))
    memory = pl.pallas_call(
        functools.partial(memory_kernel, layout),
        grid=(clips,),
        in_specs=[PLACE, text_spec, ANY, ANY, ANY, ANY],
        out_specs=pl.BlockSpec((1, TEXT_ROWS, 2 * width), lambda i: (i, 0, 0)),
        out_shape=rows((clips, TEXT_ROWS, 2 * width)),
        scratch_shapes=[pltpu.VMEM((width, 2 * width), bfloat), DMA(())],
        compiler_params=params(),
        cost_estimate=cost(6),
        name="memory",
    )(place, text_padded, *memory_all)

    gain_spec = pl.BlockSpec((1, width), lambda i: (0, 0))
    memory_spec = pl.BlockSpec((1, TEXT_ROWS, 2 * width), lambda i: (i // wins, 0, 0))
    square = pltpu.VMEM((width, width), bfloat)
    branch, lefts, cross_queries, second_sum = pl.pallas_call(
        functools.partial(cross_kernel, layout),
        grid=(windows,),
        in_specs=[
            PLACE,
            *token_specs,
            rows_spec(width),
            modulation_spec(wins, width),
            gain_spec,
            memory_spec,
            ANY,
            ANY,
            ANY,
            ANY,
        ],
        out_specs=[rows_spec(width), triple_spec, rows_spec(width), rows_spec(width)],
        out_shape=[wide_single, triple, wide, wide_single],
        scratch_shapes=[square, square, square, DMA((3,))],
        compiler_params=params(),
        cost_estimate=cost(42),
        name="cross",
    )(
        place,
        *tokens_in,
        attended,
        modulation,
        gain_full,
        memory,
        *squares_all,
    )

    window_shape = (clips, FRAMES, WS, wins, WS, width)
    piece_shape = (clips, 1, WS, wins, WS, width)
    out_specs = [whole_spec(wins, width)] + [piece_spec(wins, width, 0)] * sent
    out_shapes = [rows(window_shape)] + [rows(piece_shape)] * sent
    feed_out = pl.pallas_call(
        functools.partial(feed_kernel, layout, wins, 1024, sent),
        grid=(windows,),
        in_specs=[piece_spec(wins, width, frame) for _, frame in grad_pieces]
        + [rows_spec(width), modulation_spec(wins, width), ANY],
        out_specs=out_specs
        + [
            rows_spec(width),
            rows_spec(hidden_width),
            rows_spec(hidden_width),
            rows_spec(width),
            rows_spec(width),
            pl.BlockSpec((1, 3, width), lambda i: (i // wins, 0, 0)),
        ],
        out_shape=out_shapes
        + [
            wide,
            rows((windows, WIN_TOK, hidden_width)),
            rows((windows, WIN_TOK, hidden_width)),
            wide,
            wide_single,
            shape((clips, 3, width), single),
        ],
        scratch_shapes=[
            pltpu.VMEM((width, hidden_width), bfloat),
            pltpu.VMEM((hidden_width, width), bfloat),
            DMA((2,)),
        ],
        compiler_params=params(),
        cost_estimate=cost(117),
        name="feed",
    )(*[array for array, _ in grad_pieces], second_sum, modulation, feed_all)
    block_pieces, feed_out = feed_out[: 1 + sent], feed_out[1 + sent :]
    third_low, activated, grad_hidden, grad_reduced, grad_second_sum, feed_mod = feed_out

    def flat(values):
        return values.reshape(-1, count, values.shape[-1])

    def flat_units(values):
        return values.reshape(-1, win_count, count, columns)

    expand_of = (layout, place, flat(third_low), flat(grad_hidden), 1)
    reduce_of = (layout, place, flat(activated)[0], flat(grad_reduced)[0], 4)
    reduce_sent = layout.swap(weight_grad_rows(*reduce_of, None, "reduce_other"), "core", 1)
    expand_sent = layout.swap(weight_grad(*expand_of, None, "expand_other", True, 4), "core", 1)
    reduce_term = weight_grad_rows(*reduce_of, reduce_sent, "reduce_own")
    expand_sent, reduce_term = tie(expand_sent, reduce_term)
    expand_term = weight_grad(*expand_of, expand_sent, "expand_own", True, 4)
    grad_second_sum, expand_term = tie(grad_second_sum, expand_term)

    rights, grad_first_sum, grad_attended, grad_memory, gain_term, gate_mod = pl.pallas_call(
        functools.partial(cross_back_kernel, layout, wins),
        grid=(windows,),
        in_specs=[
            PLACE,
            *token_specs,
            modulation_spec(wins, width),
            gain_spec,
            memory_spec,
            rows_spec(width),
            rows_spec(width),
            rows_spec(width),
            ANY,
            ANY,
            ANY,
            ANY,
        ],
        out_specs=[
            units_spec,
            rows_spec(width),
            rows_spec(width),
            memory_spec,
            gain_spec,
            pl.BlockSpec((1, 1, width), lambda i: (i // wins, 0, 0)),
        ],
        out_shape=[
            units,
            wide_single,
            wide,
            shape((clips, TEXT_ROWS, 2 * width), single),
            shape((1, width), single),
            shape((clips, 1, width), single),
        ],
        scratch_shapes=[square, square, square, DMA((3,))],
        compiler_params=params(),
        cost_estimate=cost(63),
        name="cross_back",
    )(
        place,
        *tokens_in,
        modulation,
        gain_full,
        memory,
        grad_second_sum,
        cross_queries,
        branch,
        *squares_all,
    )
    reduce_stage, grad_attended = layout.reduce_axes([reduce_term], ["y"], grad_attended)
    expand_stage, grad_attended = layout.reduce_axes([expand_term], ["x"], grad_attended)
    rights, grad_memory, reduce_stage, expand_stage = tie(
        rights, grad_memory, reduce_stage, expand_stage
    )

    text_rows = text_padded.reshape(1, clips * TEXT_ROWS, width)
    memory_low = grad_memory.astype(bfloat).reshape(1, clips * TEXT_ROWS, 2 * width)
    square_of = (layout, place, flat(lefts), flat_units(rights), 1)
    memory_of = (layout, place, text_rows, memory_low, 1)
    memory_sent = weight_grad(*memory_of, None, "memory_other", split=2)
    rights, memory_sent = tie(rights, memory_sent)
    memory_sent = layout.swap(memory_sent, "core", 1)
    square_sent = weight_grad(*square_of, None, "square_other")
    masked = jnp.sum(jnp.where(null_flags[:, None, None], grad_memory, 0.0), axis=0)
    square_sent, masked = tie(square_sent, masked)
    square_sent = layout.swap(square_sent, "core", 1)
    null_term = null_text_term(layout, place, masked, memory_all)[:TXT]
    memory_sent, null_term = tie(memory_sent, null_term)
    rest_term = weight_grad(*memory_of, memory_sent, "memory_own", split=2, entries=5)
    square_sent, rest_term = tie(square_sent, rest_term)
    rest_term = weight_grad(
        *square_of, square_sent, "square_own", entries=5, into=rest_term, first=2
    )
    feed_stage, rest_term = layout.reduce_axes([expand_stage, reduce_stage], ["y", "x"], rest_term)
    grad_attended, feed_stage, rest_term, block_pieces = tie(
        grad_attended, feed_stage, rest_term, block_pieces
    )

    grad_projected, bias_sum = pl.pallas_call(
        attend_back_kernel,
        grid=(windows,),
        in_specs=[rows_spec(3 * width), rows_spec(width), PROBS_SPEC],
        out_specs=[units_spec, BIAS_SPEC],
        out_shape=[units, shape((QUADS, WIN_TOK, LANES), single)],
        scratch_shapes=[
            pltpu.VMEM((2, WIN_TOK, LANES), single),
            pltpu.VMEM((2, WIN_TOK, LANES), bfloat),
        ],
        compiler_params=params(),
        cost_estimate=cost(48),
        name="attend_back",
    )(projected, grad_attended, probs)

    feed_stage, bias_sum = layout.reduce([feed_stage], ["z"], [1], bias_sum)
    rest_stage, bias_sum = layout.reduce_axes([rest_term], ["y"], bias_sum)
    block_came, bias_sum = send_back(block_pieces[1:], win_count, bias_sum)
    grad_projected, rest_stage, feed_stage, block_came = tie(
        grad_projected, rest_stage, feed_stage, block_came
    )
    input_of = (layout, place, flat(first_low), flat_units(grad_projected), 3)
    input_sent = weight_grad(*input_of, None, "input_other", True, 3)
    input_sent = layout.swap(input_sent, "core", 1)
    input_term = weight_grad(*input_of, input_sent, "input_own", True, 3)
    bias_sum, input_term = tie(bias_sum, input_term)
    position_flat = bias_blocks(bias_sum, shift)
    for bit in range(1, layout.bits("z")):
        feed_stage, position_flat = layout.reduce([feed_stage], ["z"], [1 << bit], position_flat)
    rest_stage, position_flat = layout.reduce_axes([rest_stage], ["x"], position_flat)
    position_term = bias_collect(position_flat)
    grad_projected, rest_stage, feed_grad, position_term = tie(
        grad_projected, rest_stage, feed_stage, position_term
    )

    input_out = pl.pallas_call(
        functools.partial(input_back_kernel, layout, wins, sent),
        grid=(windows,),
        in_specs=token_specs + [modulation_spec(wins, width), units_spec, rows_spec(width), ANY],
        out_specs=out_specs + [pl.BlockSpec((1, 2, width), lambda i: (i // wins, 0, 0))],
        out_shape=out_shapes + [shape((clips, 2, width), single)],
        scratch_shapes=[pltpu.VMEM((width, 3 * width), bfloat), DMA(())],
        compiler_params=params(),
        cost_estimate=cost(29),
        name="input_back",
    )(*tokens_in, modulation, grad_projected, grad_first_sum, input_all)
    first_mod = input_out[-1]
    input_stage, first_mod = layout.reduce_axes([input_term], ["x"], first_mod)
    input_stage, first_mod = tie(input_stage, first_mod)
    rest_stage, first_mod = layout.reduce([rest_stage], ["z"], [1], first_mod)
    expand_grad = jnp.concatenate(list(feed_grad[:4]), axis=1)
    reduce_grad = feed_grad[4:].reshape(4 * depth, columns)
    heads_local = HEADS // win_count
    modulation_term = jnp.concatenate([first_mod, gate_mod, feed_mod], axis=1)
    by_columns = jnp.concatenate(
        [modulation_term.reshape(clips * 6, width), gain_term, null_term], axis=0
    )
    by_columns = by_columns.reshape(-1, win_count, columns).transpose(1, 0, 2)
    small_term = jnp.concatenate(
        [
            by_columns.reshape(win_count, -1),
            position_term.reshape(win_count, heads_local * NREL),
        ],
        axis=1,
    )
    small_term = sum_over_win(small_term, layout)
    block_whole, block_came, small_term = tie(block_pieces[0], block_came, small_term)
    block_output = put_together(block_whole, block_came, win_count)
    for bit in range(1, layout.bits("z")):
        rest_stage, small_term = layout.reduce([rest_stage], ["z"], [1 << bit], small_term)
    cross_memory_grad = jnp.concatenate([rest_stage[0], rest_stage[1]], axis=1)
    input_stage, small_term = layout.reduce_axes([input_stage], ["y"], small_term)
    modulation_grad = small_term[: clips * 6 * columns].reshape(clips, 6, columns)
    small_grad = sum_over_clip(small_term[clips * 6 * columns :], layout, 1, clip_size // 2)
    tokens_came, small_grad = send_back(input_out[1 : 1 + sent], win_count, small_grad)
    tokens_grad = put_together(input_out[0], tokens_came, win_count)
    input_stage, small_grad = layout.reduce([input_stage], ["z"], [1], small_grad)
    small_grad = sum_over_clip(small_grad, layout, clip_size // 2, clip_size)
    gain_grad = small_grad[:columns]
    null_grad = small_grad[columns : (1 + TXT) * columns].reshape(TXT, columns)
    position_grad = small_grad[(1 + TXT) * columns :].reshape(heads_local, NREL)
    for bit in range(1, layout.bits("z")):
        input_stage, small_grad = layout.reduce([input_stage], ["z"], [1 << bit], small_grad)
    self_input_grad = jnp.concatenate(list(input_stage), axis=1)
    self_output_grad, cross_query_grad, cross_output_grad = rest_stage[2:]
    return (
        block_output,
        tokens_grad,
        self_input_grad,
        self_output_grad,
        cross_query_grad,
        cross_memory_grad,
        cross_output_grad,
        expand_grad,
        reduce_grad,
        gain_grad,
        null_grad,
        position_grad,
        modulation_grad,
    )


def solution(mesh):
    in_specs = (
        P("clip", "win", None),
        P("clip", "win", None),
        P("clip", None, None),
        P("clip", None, None),
        P("clip"),
        P(None, "win"),
        P("win"),
        P("win", None),
        P("clip", "win"),
        P("clip", "win"),
        P("clip", "win"),
        P("clip", "win"),
        P("clip", "win"),
        P("clip", "win"),
        P("clip", "win"),
    )
    out_specs = (
        P("clip", "win", None),
        P("clip", "win", None),
        P("clip", "win"),
        P("clip", "win"),
        P("clip", "win"),
        P("clip", "win"),
        P("clip", "win"),
        P("clip", "win"),
        P("clip", "win"),
        P("win"),
        P(None, "win"),
        P("win", None),
        P("clip", None, "win"),
    )
    return jax.shard_map(local, mesh=mesh, in_specs=in_specs, out_specs=out_specs, check_vma=False)
```

```python
import functools
import math

import jax
import jax.numpy as jnp
from jax import lax
from jax.experimental import pallas as pl
from jax.experimental.pallas import tpu as pltpu
from jax.sharding import PartitionSpec as P

HEADS = 16
HD = 64
FRAMES = 5
GRID = 32
WS = 8
SEQ = 5120
WIN_TOK = 320
NREL = 2025
TXT = 77
QUAD = 4
QW = QUAD * HD
QUADS = HEADS // QUAD
SPAN = 2 * WS - 1
FSPAN = 2 * FRAMES - 1
SIDE = WS * WS
PAIR = 2 * HD
LANES = QUAD * WIN_TOK
TEXT_ROWS = 80
CHUNK = 256

epsilon = 1e-06
gelu_coefficient = 0.7978845608028654
scale_factor = HD ** (-0.5)
bfloat = jnp.bfloat16
single = jnp.float32
NEGATIVE = -1e30
VMEM_LIMIT = 60 * 1024 * 1024

NN = (((1,), (0,)), ((), ()))
NT = (((1,), (1,)), ((), ()))
TN = (((0,), (0,)), ((), ()))


def mm(left, right, dims=NN):
    return lax.dot_general(left, right, dims, preferred_element_type=single)


def norm_parts(values):
    centered = values - jnp.mean(values, axis=-1, keepdims=True)
    variance = jnp.mean(centered * centered, axis=-1, keepdims=True)
    inverse = lax.rsqrt(variance + epsilon)
    return centered * inverse, inverse


def norm_back(normed, inverse, grad):
    return inverse * (
        grad
        - jnp.mean(grad, axis=-1, keepdims=True)
        - normed * jnp.mean(grad * normed, axis=-1, keepdims=True)
    )


def params():
    return pltpu.CompilerParams(vmem_limit_bytes=VMEM_LIMIT)


def cost(microseconds):
    return pl.CostEstimate(
        flops=int(microseconds * 760e9),
        bytes_accessed=int(microseconds * 1e9),
        transcendentals=0,
    )


def tie(*values):
    return lax.optimization_barrier(values)


ANY = pl.BlockSpec(memory_space=pl.ANY)
PLACE = pl.BlockSpec(memory_space=pltpu.SMEM)
FIRST_ORDER = ("z", "x", "y")
OTHER_ORDER = ("z", "y", "x")


class Term:
    def __init__(self, kept, sent, lead):
        self.kept, self.sent, self.lead = kept, sent, lead


jax.tree_util.register_pytree_node(
    Term, lambda t: ((t.kept, t.sent), t.lead), lambda lead, parts: Term(*parts, lead)
)


class Layout:
    def __init__(self, clip_size, win_count):
        self.clip_size, self.win_count = clip_size, win_count
        y = 2 ** ((clip_size.bit_length() - 1) // 2)
        self.size = {"z": clip_size // y, "y": y, "x": win_count // 2, "core": 2}
        self.home = {"z": "clip", "y": "clip", "x": "win", "core": "win"}
        self.stride = {"z": y, "y": 1, "x": 2, "core": 1}
        self.others = clip_size * win_count // 2

    def place(self):
        clip, win = lax.axis_index("clip"), lax.axis_index("win")
        y = self.size["y"]
        return jnp.stack([clip // y, clip % y, win // 2, win % 2]).astype(jnp.int32)

    def swap(self, values, axis, apart):
        home = self.home[axis]
        count = self.clip_size if home == "clip" else self.win_count
        step = apart * self.stride[axis]
        return lax.ppermute(values, home, [(i, i ^ step) for i in range(count)])

    def gather(self, held, axis, apart, pin):
        part, pin = tie(self.swap(held, axis, apart), pin)
        return held, part, pin

    def gather_axis(self, held, axis, pin):
        apart = 1
        while apart < self.size[axis]:
            held, part, pin = self.gather(held, axis, apart, pin)
            held = jnp.concatenate([held, part], axis=0)
            apart *= 2
        return held, pin

    def gather_last(self, held, axis, pin):
        apart = 1
        while apart < self.size[axis] // 2:
            held, part, pin = self.gather(held, axis, apart, pin)
            held = jnp.concatenate([held, part], axis=0)
            apart *= 2
        return self.gather(held, axis, apart, pin)

    def with_other_core(self, *arrays):
        return list(arrays) + [self.swap(array, "core", 1) for array in arrays]

    def owner(self, place_ref, order, index, core_apart):
        names = ("z", "y", "x", "core")
        at = {name: place_ref[i] for i, name in enumerate(names)}
        for axis in order:
            at[axis] = at[axis] ^ (index % self.size[axis])
            index = index // self.size[axis]
        core = at["core"] ^ core_apart
        return at["z"] * self.size["y"] + at["y"], at["x"] * 2 + core

    def reduce(self, terms, axes, apart, pin):
        came, pin = self.exchange(terms, axes, apart, pin)
        return self.combine(terms, came), pin

    def exchange(self, terms, axes, apart, pin):
        came = [self.swap(term.sent, axis, n) for term, axis, n in zip(terms, axes, apart)]
        return tie(came, pin)

    def combine(self, terms, came):
        pairs = []
        for term, part in zip(terms, came):
            kept, lead = term.kept, term.lead
            while lead > 0 and kept.shape[0] == 1:
                kept, part, lead = kept[0], part[0], lead - 1
            pairs.append((kept, part))
        if lead == 0:
            sums = [kept.astype(single) + part.astype(single) for kept, part in pairs]
            return jnp.concatenate(sums, axis=0)
        return Term(*add_halves(pairs), lead)

    def reduce_axes(self, terms, axes, pin):
        terms = list(terms)
        for i, axis in enumerate(axes):
            for bit in range(self.bits(axis) - 1):
                terms[i], pin = self.reduce([terms[i]], [axis], [1 << bit], pin)
        return self.reduce(terms, axes, [self.size[axis] // 2 for axis in axes], pin)

    def bits(self, axis):
        return self.size[axis].bit_length() - 1


def add_kernel(*refs):
    ins, outs, at = refs[:-2], refs[-2:], 0
    for i in range(0, len(ins), 2):
        count = ins[i].shape[2]
        for half, out_ref in enumerate(outs):
            total = ins[i][half, 0].astype(single) + ins[i + 1][half, 0].astype(single)
            out_ref[0, at : at + count] = total.astype(bfloat)
        at += count


def add_halves(pairs):
    shape = pairs[0][0].shape
    lead = (shape[0] // 2,) + shape[1:-3]
    steps, total = math.prod(lead), sum(kept.shape[-3] for kept, _ in pairs)
    ins, in_specs = [], []
    for pair in pairs:
        tail = pair[0].shape[-3:]
        ins += [array.reshape((2, steps) + tail) for array in pair]
        in_specs += [pl.BlockSpec((2, 1) + tail, lambda i: (0, i, 0, 0, 0))] * 2
    tail = (total,) + shape[-2:]
    outs = pl.pallas_call(
        add_kernel,
        grid=(steps,),
        in_specs=in_specs,
        out_specs=[pl.BlockSpec((1,) + tail, lambda i: (i, 0, 0, 0))] * 2,
        out_shape=[jax.ShapeDtypeStruct((steps,) + tail, bfloat)] * 2,
        compiler_params=params(),
        cost_estimate=cost(0),
        name="add_halves",
    )(*ins)
    return [out.reshape(lead + tail) for out in outs]


def reverse(index, size):
    distance, bits = 0, size.bit_length() - 1
    for b in range(bits):
        distance = distance + (((index >> b) & 1) << (bits - 1 - b))
    return distance


def start_weight(sources, target, sem, layout, place_ref, order, cols, offset=0):
    half = len(sources) // 2
    for k, source in enumerate(sources):
        count, rows = source.shape[:2]

        def step(i, carry, source=source, k=k, count=count, rows=rows):
            clip, win = layout.owner(place_ref, order, i + k % half * count, k // half)
            row = pl.multiple_of(clip * rows, rows)
            column = pl.multiple_of(win * cols, cols)
            pltpu.make_async_copy(
                source.at[i, :, pl.ds(offset, cols)],
                target.at[pl.ds(row, rows), pl.ds(column, cols)],
                sem,
            ).start()
            return carry

        lax.fori_loop(0, count, step, 0)


def start_squares(sources, targets, sems, layout, place_ref):
    cols = sources[0].shape[2] // len(targets)
    for i, target in enumerate(targets):
        start_weight(sources, target, sems.at[i], layout, place_ref, FIRST_ORDER, cols, i * cols)


def start_gathered(source, target, sem, layout, cols, offset=0):
    depth = source.shape[1]
    rows = target.shape[0] // layout.clip_size

    def step(c, carry):
        for w in range(layout.win_count):
            for piece in range(rows // depth):
                row = pl.multiple_of(c * rows + piece * depth, depth)
                pltpu.make_async_copy(
                    source.at[c * layout.win_count + w, :, pl.ds(offset + piece * cols, cols)],
                    target.at[pl.ds(row, depth), pl.ds(w * cols, cols)],
                    sem,
                ).start()
        return carry

    lax.fori_loop(0, layout.clip_size, step, 0)


def wait_weight(target, sem):
    pltpu.make_async_copy(target, target, sem).wait()


def piece_spec(wins, width, frame):
    return pl.BlockSpec(
        (1, 1, WS, 1, WS, width), lambda i: (i // wins, frame, 0, i % wins, 0, 0)
    )


def whole_spec(wins, width):
    return pl.BlockSpec(
        (1, FRAMES, WS, 1, WS, width), lambda i: (i // wins, 0, 0, i % wins, 0, 0)
    )


def rows_spec(width):
    return pl.BlockSpec((1, WIN_TOK, width), lambda i: (i, 0, 0))


def modulation_spec(wins, width):
    return pl.BlockSpec((1, 6, width), lambda i: (i // wins, 0, 0))


def load_window(refs):
    parts = [ref[0, 0, :, 0].astype(single).reshape(SIDE, ref.shape[-1]) for ref in refs]
    return jnp.concatenate(parts, axis=0)


def store_window(refs, values):
    whole, others = refs[0], refs[1:]
    shape = (FRAMES, WS, WS, whole.shape[-1])
    values = values.reshape(shape).astype(whole.dtype)
    if not others:
        whole[0, :, :, 0] = values
        return
    whole[0, 0, :, 0] = values[0]
    whole[0, FRAMES - 1, :, 0] = values[1]
    for i, other in enumerate(others):
        other[0, 0, :, 0] = values[2 + i]


def store_units(ref, index, first, values):
    unit = ref.shape[-1]
    for at in range(0, values.shape[1], unit):
        ref[index, (first + at) // unit, 0] = values[:, at : at + unit]


def frame_offset(shift, query, key):
    return lax.rem(shift + query, FRAMES) - lax.rem(shift + key, FRAMES) + FRAMES - 1


def frame_blocks():
    for key in range(FRAMES):
        for query in range(FRAMES):
            for pair in range(QUAD // 2):
                lane = query * QW + pair * PAIR
                yield key, query, pair, slice(key * SIDE, (key + 1) * SIDE), slice(lane, lane + PAIR)


def table_kernel(shift_ref, block_ref, out_ref):
    for key, query, pair, rows, lanes in frame_blocks():
        offset = frame_offset(shift_ref[0], query, key)
        out_ref[0, rows, lanes] = block_ref[pair, offset]


def collect_kernel(shift_ref, sum_ref, out_ref, pairs_ref):
    pairs_ref[...] = jnp.zeros(pairs_ref.shape, single)
    for key, query, pair, rows, lanes in frame_blocks():
        offset = frame_offset(shift_ref[0], query, key)
        pairs_ref[pair, offset] += sum_ref[0, rows, lanes]
    for head in range(QUAD):
        lanes = slice(head % 2 * HD, (head % 2 + 1) * HD)
        out_ref[head] = pairs_ref[head // 2, :, :, lanes]


QUAD_SPEC = pl.BlockSpec((1, WIN_TOK, LANES), lambda q, s: (q, 0, 0))
BLOCKS_SPEC = pl.BlockSpec((QUAD // 2, FSPAN, SIDE, PAIR), lambda q, s: (q, 0, 0, 0))


def side_hot():
    shape = (SPAN * SPAN, SIDE * SIDE)
    offset = lax.broadcasted_iota(jnp.int32, shape, 0)
    pair = lax.broadcasted_iota(jnp.int32, shape, 1)
    key, query = pair // SIDE, pair % SIDE
    rows = query // WS - key // WS + WS - 1
    columns = query % WS - key % WS + WS - 1
    return (rows * SPAN + columns == offset).astype(single)


def table_blocks(bias_full):
    flat = bias_full.reshape(HEADS * FSPAN, SPAN * SPAN)
    blocks = jnp.dot(flat, side_hot(), precision=lax.Precision.HIGHEST)
    blocks = blocks.reshape(HEADS // 2, 2, FSPAN, SIDE, SIDE).transpose(0, 2, 3, 1, 4)
    return blocks.reshape(HEADS // 2, FSPAN, SIDE, PAIR)


def bias_table(blocks, shift):
    return pl.pallas_call(
        table_kernel,
        grid_spec=pltpu.PrefetchScalarGridSpec(
            num_scalar_prefetch=1,
            grid=(QUADS,),
            in_specs=[BLOCKS_SPEC],
            out_specs=QUAD_SPEC,
        ),
        out_shape=jax.ShapeDtypeStruct((QUADS, WIN_TOK, LANES), single),
        compiler_params=params(),
        cost_estimate=cost(5),
        name="bias_table",
    )(shift, blocks)


def bias_blocks(bias_sum, shift):
    return pl.pallas_call(
        collect_kernel,
        grid_spec=pltpu.PrefetchScalarGridSpec(
            num_scalar_prefetch=1,
            grid=(QUADS,),
            in_specs=[QUAD_SPEC],
            out_specs=pl.BlockSpec((QUAD, FSPAN, SIDE, SIDE), lambda q, s: (q, 0, 0, 0)),
            scratch_shapes=[pltpu.VMEM((QUAD // 2, FSPAN, SIDE, PAIR), single)],
        ),
        out_shape=jax.ShapeDtypeStruct((HEADS, FSPAN, SIDE, SIDE), single),
        compiler_params=params(),
        cost_estimate=cost(5),
        name="bias_collect",
    )(shift, bias_sum).reshape(HEADS * FSPAN, SIDE * SIDE)


def bias_collect(flat):
    summed = lax.dot_general(flat, side_hot(), NT, precision=lax.Precision.HIGHEST)
    return summed.reshape(HEADS, NREL)


def project_kernel(layout, *refs):
    token_refs, refs = refs[:FRAMES], refs[FRAMES:]
    mod_ref, weight_any, low_ref, out_ref, weight_ref, sem = refs

    @pl.when(pl.program_id(0) == 0)
    def _():
        start_gathered(weight_any, weight_ref, sem, layout, weight_any.shape[2])
        wait_weight(weight_ref, sem)

    normed, _ = norm_parts(load_window(token_refs))
    low = (normed * (1.0 + mod_ref[0, 1:2]) + mod_ref[0, 0:1]).astype(bfloat)
    low_ref[0] = low
    out_ref[0] = mm(low, weight_ref[...]).astype(bfloat)


def head_mask(rows, head):
    lane = lax.broadcasted_iota(jnp.int32, (rows, QW), 1)
    return (lane >= head * HD) & (lane < (head + 1) * HD)


def spread(values):
    masks = [head_mask(SIDE, h) for h in range(QUAD)]
    parts = []
    for frame in range(FRAMES):
        rows = values[frame * SIDE : (frame + 1) * SIDE]
        parts += [jnp.where(mask, rows, jnp.zeros_like(rows)) for mask in masks]
    return jnp.concatenate(parts, axis=0)


def own_heads(product):
    lane = lax.broadcasted_iota(jnp.int32, (SIDE, PAIR), 1)
    rows = []
    for frame in range(FRAMES):
        parts = []
        for pair in range(QUAD // 2):
            at = frame * QW + pair * PAIR
            block = product[pair * PAIR : (pair + 1) * PAIR, at : at + PAIR].T
            parts.append(jnp.where(lane < HD, block[:SIDE], block[SIDE:]))
        rows.append(jnp.concatenate(parts, axis=1))
    return jnp.concatenate(rows, axis=0)


def softmax_down(scores):
    expanded = jnp.exp(scores - jnp.max(scores, axis=0, keepdims=True))
    return expanded * (1.0 / jnp.sum(expanded, axis=0, keepdims=True))


def lane_chunks():
    return [slice(c, c + CHUNK) for c in range(0, LANES, CHUNK)]


def attend_kernel(projected_ref, bias_ref, out_ref, probs_ref, scores_ref):
    width = out_ref.shape[-1]
    for q in range(QUADS):
        at, slot = slice(q * QW, (q + 1) * QW), q % 2
        queries = spread(projected_ref[0, :, at] * jnp.asarray(scale_factor, bfloat))
        keys = projected_ref[0, :, width + q * QW : width + (q + 1) * QW]
        values = projected_ref[0, :, 2 * width + q * QW : 2 * width + (q + 1) * QW]
        scores_ref[slot] = mm(keys, queries, NT)
        for lanes in lane_chunks():
            scores = scores_ref[slot, :, lanes] + bias_ref[q, :, lanes]
            probs_ref[0, q, :, lanes] = softmax_down(scores).astype(bfloat)
        out_ref[0, :, at] = own_heads(mm(values, probs_ref[0, q], TN)).astype(bfloat)


def attend_back_kernel(
    projected_ref, grad_ref, probs_ref, out_ref, sum_ref, grad_probs_ref, grad_scores_ref
):
    @pl.when(pl.program_id(0) == 0)
    def _():
        sum_ref[...] = jnp.zeros(sum_ref.shape, single)

    width = grad_ref.shape[-1]
    for q in range(QUADS):
        at, slot = slice(q * QW, (q + 1) * QW), q % 2
        queries = spread(projected_ref[0, :, at] * jnp.asarray(scale_factor, bfloat))
        keys = projected_ref[0, :, width + q * QW : width + (q + 1) * QW]
        values = projected_ref[0, :, 2 * width + q * QW : 2 * width + (q + 1) * QW]
        grads = spread(grad_ref[0, :, at])
        grad_probs_ref[slot] = mm(values, grads, NT)
        store_units(out_ref, 2, q * QW, mm(probs_ref[0, q], grads).astype(bfloat))
        for lanes in lane_chunks():
            probs = probs_ref[0, q, :, lanes].astype(single)
            weighted = probs * grad_probs_ref[slot, :, lanes]
            grad_scores = weighted - probs * jnp.sum(weighted, axis=0, keepdims=True)
            grad_scores_ref[slot, :, lanes] = grad_scores.astype(bfloat)
            sum_ref[q, :, lanes] += grad_scores
        store_units(out_ref, 1, q * QW, mm(grad_scores_ref[slot], queries).astype(bfloat))
        grad_queries = own_heads(mm(keys, grad_scores_ref[slot], TN))
        store_units(out_ref, 0, q * QW, (grad_queries * scale_factor).astype(bfloat))


BIAS_SPEC = pl.BlockSpec((QUADS, WIN_TOK, LANES), lambda i: (0, 0, 0))
PROBS_SPEC = pl.BlockSpec((1, QUADS, WIN_TOK, LANES), lambda i: (i, 0, 0, 0))


def memory_kernel(layout, place_ref, text_ref, *refs):
    sources, (memory_ref, weight_ref, sem) = refs[:4], refs[4:]

    @pl.when(pl.program_id(0) == 0)
    def _():
        cols = sources[0].shape[2]
        start_weight(sources, weight_ref, sem, layout, place_ref, OTHER_ORDER, cols)
        wait_weight(weight_ref, sem)

    memory_ref[0] = mm(text_ref[0], weight_ref[...]).astype(bfloat)


def cross_probs(queries, keys):
    scores = mm(keys, queries, NT)
    whole = TXT // 8 * 8
    row = lax.broadcasted_iota(jnp.int32, (TEXT_ROWS - whole, LANES), 0) + whole
    rest = jnp.where(row < TXT, scores[whole:], NEGATIVE)
    return softmax_down(jnp.concatenate([scores[:whole], rest], axis=0))


def cross_kernel(layout, place_ref, *refs):
    token_refs, refs = refs[:FRAMES], refs[FRAMES:]
    attended_ref, mod_ref, gain_ref, memory_ref = refs[:4]
    sources, refs = refs[4:8], refs[8:]
    branch_ref, left_ref, queries_ref, sum_ref, output_ref, query_ref, cross_ref, sems = refs

    @pl.when(pl.program_id(0) == 0)
    def _():
        start_squares(sources, (output_ref, query_ref, cross_ref), sems, layout, place_ref)
        wait_weight(output_ref, sems.at[0])
        wait_weight(query_ref, sems.at[1])
        wait_weight(cross_ref, sems.at[2])

    attended = attended_ref[0]
    left_ref[0, 0] = attended
    branch = mm(attended, output_ref[...])
    branch_ref[0] = branch
    first_sum = load_window(token_refs) + mod_ref[0, 2:3] * branch
    normed, _ = norm_parts(first_sum)
    second = (normed * gain_ref[...]).astype(bfloat)
    left_ref[1, 0] = second
    queries = mm(second, query_ref[...]).astype(bfloat)
    queries_ref[0] = queries
    width = queries.shape[1]
    parts = []
    for q in range(QUADS):
        at = slice(q * QW, (q + 1) * QW)
        scaled = spread(queries[:, at] * jnp.asarray(scale_factor, bfloat))
        probs = cross_probs(scaled, memory_ref[0, :, at]).astype(bfloat)
        values = memory_ref[0, :, width + q * QW : width + (q + 1) * QW]
        parts.append(own_heads(mm(values, probs, TN)).astype(bfloat))
    crossed = jnp.concatenate(parts, axis=1)
    left_ref[2, 0] = crossed
    sum_ref[0] = first_sum + mm(crossed, cross_ref[...])


def cross_back_kernel(layout, wins, place_ref, *refs):
    token_refs, refs = refs[:FRAMES], refs[FRAMES:]
    mod_ref, gain_ref, memory_ref, grad_ref, queries_ref, branch_ref = refs[:6]
    sources, refs = refs[6:10], refs[10:]
    right_ref, grad_sum_ref, grad_attended_ref = refs[:3]
    grad_memory_ref, gain_grad_ref, gate_grad_ref = refs[3:6]
    output_ref, query_ref, cross_ref, sems = refs[6:]
    step = pl.program_id(0)

    @pl.when(step == 0)
    def _():
        start_squares(sources, (output_ref, query_ref, cross_ref), sems, layout, place_ref)
        wait_weight(output_ref, sems.at[0])
        wait_weight(query_ref, sems.at[1])
        wait_weight(cross_ref, sems.at[2])
        gain_grad_ref[...] = jnp.zeros(gain_grad_ref.shape, single)

    @pl.when(step % wins == 0)
    def _():
        grad_memory_ref[...] = jnp.zeros(grad_memory_ref.shape, single)
        gate_grad_ref[...] = jnp.zeros(gate_grad_ref.shape, single)

    width = queries_ref.shape[-1]
    grad = grad_ref[0]
    grad_low = grad.astype(bfloat)
    store_units(right_ref, 2, 0, grad_low)
    grad_crossed = mm(grad_low, cross_ref[...], NT).astype(bfloat)
    queries = queries_ref[0]
    query_parts = []
    for q in range(QUADS):
        at = slice(q * QW, (q + 1) * QW)
        value_at = slice(width + q * QW, width + (q + 1) * QW)
        scaled = spread(queries[:, at] * jnp.asarray(scale_factor, bfloat))
        grads = spread(grad_crossed[:, at])
        keys = memory_ref[0, :, at]
        probs = cross_probs(scaled, keys)
        weighted = probs * mm(memory_ref[0, :, value_at], grads, NT)
        grad_scores = weighted - probs * jnp.sum(weighted, axis=0, keepdims=True)
        grad_scores = grad_scores.astype(bfloat)
        grad_memory_ref[0, :, at] += mm(grad_scores, scaled)
        grad_memory_ref[0, :, value_at] += mm(probs.astype(bfloat), grads)
        part = own_heads(mm(keys, grad_scores, TN))
        query_parts.append((part * scale_factor).astype(bfloat))
    grad_queries = jnp.concatenate(query_parts, axis=1)
    store_units(right_ref, 1, 0, grad_queries)
    grad_second = mm(grad_queries, query_ref[...], NT)
    branch = branch_ref[0]
    normed, inverse = norm_parts(load_window(token_refs) + mod_ref[0, 2:3] * branch)
    gain_grad_ref[...] += jnp.sum(grad_second * normed, axis=0, keepdims=True)
    grad_sum = grad + norm_back(normed, inverse, grad_second * gain_ref[...])
    grad_sum_ref[0] = grad_sum
    gate_grad_ref[0] += jnp.sum(grad_sum * branch, axis=0, keepdims=True)
    grad_branch = (mod_ref[0, 2:3] * grad_sum).astype(bfloat)
    store_units(right_ref, 0, 0, grad_branch)
    grad_attended_ref[0] = mm(grad_branch, output_ref[...], NT).astype(bfloat)


def null_kernel(layout, place_ref, masked_ref, *refs):
    sources, (out_ref, weight_ref, sem) = refs[:4], refs[4:]
    cols = sources[0].shape[2]
    start_weight(sources, weight_ref, sem, layout, place_ref, OTHER_ORDER, cols)
    wait_weight(weight_ref, sem)
    masked = masked_ref[...]
    high = masked.astype(bfloat)
    rest = (masked - high.astype(single)).astype(bfloat)
    weight = weight_ref[...]
    out_ref[...] = mm(high, weight, NT) + mm(rest, weight, NT)


def null_text_term(layout, place, masked, sources):
    width = masked.shape[1] // 2
    whole = pl.BlockSpec(memory_space=pltpu.VMEM)
    return pl.pallas_call(
        functools.partial(null_kernel, layout),
        in_specs=[PLACE, whole, ANY, ANY, ANY, ANY],
        out_specs=whole,
        out_shape=jax.ShapeDtypeStruct((masked.shape[0], width), single),
        scratch_shapes=[pltpu.VMEM((width, 2 * width), bfloat), pltpu.SemaphoreType.DMA(())],
        compiler_params=params(),
        cost_estimate=cost(5),
        name="null_text",
    )(place, masked, *sources)


def feed_kernel(layout, wins, chunk, sent, *refs):
    grad_out_refs, refs = refs[:FRAMES], refs[FRAMES:]
    sum_ref, mod_ref, weights_any = refs[:3]
    out_refs, refs = refs[3 : 4 + sent], refs[4 + sent :]
    third_ref, act_ref, grad_hidden_ref, grad_reduced_ref, grad_sum_ref, grad_mod_ref = refs[:6]
    expand_ref, reduce_ref, sems = refs[6:]
    step = pl.program_id(0)

    @pl.when(step == 0)
    def _():
        cols = expand_ref.shape[1] // layout.win_count
        start_gathered(weights_any, expand_ref, sems.at[0], layout, cols)
        offset = cols
        cols = reduce_ref.shape[1] // layout.win_count
        start_gathered(weights_any, reduce_ref, sems.at[1], layout, cols, offset)
        wait_weight(expand_ref, sems.at[0])
        wait_weight(reduce_ref, sems.at[1])

    @pl.when(step % wins == 0)
    def _():
        grad_mod_ref[...] = jnp.zeros(grad_mod_ref.shape, single)

    second_sum = sum_ref[0]
    normed, inverse = norm_parts(second_sum)
    third = (normed * (1.0 + mod_ref[0, 4:5]) + mod_ref[0, 3:4]).astype(bfloat)
    third_ref[0] = third
    grad_out = load_window(grad_out_refs)
    gate = mod_ref[0, 5:6]
    grad_reduced = (gate * grad_out).astype(bfloat)
    grad_reduced_ref[0] = grad_reduced
    hidden_width = expand_ref.shape[1]
    for at in range(0, hidden_width, chunk):
        part = slice(at, at + chunk)
        v = mm(third, expand_ref[:, part])
        grad_act = mm(grad_reduced, reduce_ref[part], NT)
        square = v * v
        tanh = jnp.tanh(gelu_coefficient * (v + 0.044715 * (square * v)))
        half = 0.5 * (1.0 + tanh)
        act_ref[0, :, part] = (v * half).astype(bfloat)
        slope = half + (0.5 * gelu_coefficient) * v * (1.0 - tanh * tanh) * (
            1.0 + (3 * 0.044715) * square
        )
        grad_hidden_ref[0, :, part] = (grad_act * slope).astype(bfloat)
    reduced = mm(act_ref[0], reduce_ref[...])
    store_window(out_refs, second_sum + gate * reduced)
    grad_third = mm(grad_hidden_ref[0], expand_ref[...], NT)
    grad_mod_ref[0, 0:1] += jnp.sum(grad_third, axis=0, keepdims=True)
    grad_mod_ref[0, 1:2] += jnp.sum(grad_third * normed, axis=0, keepdims=True)
    grad_mod_ref[0, 2:3] += jnp.sum(grad_out * reduced, axis=0, keepdims=True)
    grad_sum_ref[0] = grad_out + norm_back(normed, inverse, grad_third * (1.0 + mod_ref[0, 4:5]))


def input_back_kernel(layout, wins, sent, *refs):
    token_refs, refs = refs[:FRAMES], refs[FRAMES:]
    mod_ref, grad_ref, grad_sum_ref, weight_any = refs[:4]
    out_refs, (grad_mod_ref, weight_ref, sem) = refs[4 : 5 + sent], refs[5 + sent :]
    step = pl.program_id(0)

    @pl.when(step == 0)
    def _():
        start_gathered(weight_any, weight_ref, sem, layout, weight_any.shape[2])
        wait_weight(weight_ref, sem)

    @pl.when(step % wins == 0)
    def _():
        grad_mod_ref[...] = jnp.zeros(grad_mod_ref.shape, single)

    units = [grad_ref[k, u, 0] for k in range(3) for u in range(grad_ref.shape[1])]
    grads = jnp.concatenate(units, axis=1)
    grad_first = mm(grads, weight_ref[...], NT)
    normed, inverse = norm_parts(load_window(token_refs))
    grad_mod_ref[0, 0:1] += jnp.sum(grad_first, axis=0, keepdims=True)
    grad_mod_ref[0, 1:2] += jnp.sum(grad_first * normed, axis=0, keepdims=True)
    back = norm_back(normed, inverse, grad_first * (1.0 + mod_ref[0, 1:2]))
    store_window(out_refs, grad_sum_ref[0] + back)


def owner_column(layout, place_ref, step, core_apart):
    distance = reverse(step, layout.size["x"])
    return (place_ref[2] ^ distance) * 2 + (place_ref[3] ^ core_apart)


def owner_row(layout, place_ref, y, z):
    y, z = reverse(y, layout.size["y"]), reverse(z, layout.size["z"])
    return (place_ref[0] ^ z) * layout.size["y"] + (place_ref[1] ^ y)


def columns_kernel(layout, pieces, added, x_first, pair, place_ref, x_ref, *refs):
    outs = 2 if pair else 1
    y_refs, out_refs, product_ref = refs[:pieces], refs[-1 - outs : -1], refs[-1]
    split, rows, width = out_refs[0].shape[-3:]
    cols = product_ref.shape[1] // pieces
    for i in range(pieces):
        product_ref[:, i * cols : (i + 1) * cols] = mm(x_ref[0], y_refs[i][0], TN)

    def store(out_ref, first_y, last_y):
        for y in range(first_y, last_y):
            for z in range(layout.size["z"]):
                clip = owner_row(layout, place_ref, y, z)
                part = product_ref[pl.ds(pl.multiple_of(clip * rows, rows), rows)]
                for i in range(split):
                    piece = part[:, i * width : (i + 1) * width]
                    if added:
                        at = (0, y, z, i) if x_first else (y, 0, z, i)
                        piece = piece + refs[pieces][at].astype(single)
                    at = (0, y, z, i) if x_first else (y - first_y, 0, z, i)
                    out_ref[at] = piece.astype(bfloat)

    size_y = layout.size["y"]
    if not pair:
        store(out_refs[0], 0, size_y)
    elif x_first:
        half = layout.size["x"] // 2
        pl.when(pl.program_id(1) < half)(lambda: store(out_refs[0], 0, size_y))
        pl.when(pl.program_id(1) >= half)(lambda: store(out_refs[1], 0, size_y))
    else:
        store(out_refs[0], 0, size_y // 2)
        store(out_refs[1], size_y // 2, size_y)


def weight_grad(
    layout, place, x, y, pieces, added, name, x_first=False, split=1, entries=None, into=None, first=0
):
    pair = added is not None
    core_apart = 0 if pair else 1
    count, tokens, depth = x.shape
    unit = y.shape[-1] if y.ndim == 4 else y.shape[-1] // layout.win_count
    rows, cols = depth // layout.clip_size, pieces * unit
    size = layout.size

    def unit_spec(i):
        def index(n, j, place_ref):
            at = owner_column(layout, place_ref, j, core_apart) * pieces + i
            return (n * pieces + at // layout.win_count, 0, at % layout.win_count)

        if y.ndim == 3:
            return pl.BlockSpec((1, tokens, unit), index)

        def unit_index(n, j, place_ref):
            entry, _, at = index(n, j, place_ref)
            return (entry, at, 0, 0)

        return pl.BlockSpec((1, None, tokens, unit), unit_index)

    axes = ("x", "y", "z") if x_first else ("y", "x", "z")
    leading = tuple(size[axis] for axis in axes)
    half = leading[0] // 2

    def block(start, part):
        step = size["x"] if part is None else half
        lead = (1,) + leading[1:] if x_first else (leading[0] if part is None else half, 1, size["z"])

        def index(n, j, place_ref):
            at = n + start // split
            if not x_first:
                return (0, j, 0, at, 0, 0)
            if part is not None:
                j = jnp.clip(j - part * half, 0, step - 1)
            return (j, 0, 0, at, 0, 0)

        return pl.BlockSpec(lead + (split, rows, cols // split), index)

    if pair:
        out_specs = [block(first, 0), block(first, 1)]
        total = entries or count * split
        out_lead = (half,) + leading[1:]
    else:
        out_specs = [block(0, None)]
        total, out_lead = count * split, leading
    extra = ([added] if pair else []) + ([into.kept, into.sent] if into else [])
    extra_specs = ([block(0, None)] if pair else []) + ([ANY, ANY] if into else [])
    start = 2 + pieces + (1 if pair else 0)
    out_shape = jax.ShapeDtypeStruct(out_lead + (total, rows, cols // split), bfloat)
    outs = pl.pallas_call(
        functools.partial(columns_kernel, layout, pieces, pair, x_first, pair),
        grid_spec=pltpu.PrefetchScalarGridSpec(
            num_scalar_prefetch=1,
            grid=(count, size["x"]),
            in_specs=[pl.BlockSpec((1, tokens, depth), lambda n, j, p: (n, 0, 0))]
            + [unit_spec(i) for i in range(pieces)]
            + extra_specs,
            out_specs=out_specs,
            scratch_shapes=[pltpu.VMEM((depth, cols), single)],
        ),
        out_shape=[out_shape] * len(out_specs),
        input_output_aliases={start: 0, start + 1: 1} if into else {},
        compiler_params=params(),
        cost_estimate=cost(count * size["x"] * tokens * depth * cols / 382e3),
        name=name,
    )(place, x, *([y] * pieces), *extra)
    return Term(outs[0], outs[1], 3) if pair else outs[0]


def rows_kernel(layout, pair, place_ref, x_ref, *refs):
    size = layout.size["x"]
    y_refs, out_refs = refs[:size], refs[-2 if pair else -1 :]
    left = x_ref[...]

    def store(out_ref):
        for j in range(size):
            part = mm(left, y_refs[j][...], TN).reshape(out_ref.shape[3:])
            if pair:
                part = part + refs[size][0, j, 0].astype(single)
            out_ref[0, j, 0] = part.astype(bfloat)

    if not pair:
        store(out_refs[0])
        return
    half = layout.size["y"] // 2
    pl.when(pl.program_id(0) < half)(lambda: store(out_refs[0]))
    pl.when(pl.program_id(0) >= half)(lambda: store(out_refs[1]))


def weight_grad_rows(layout, place, x, y, split, added, name):
    tokens, depth = x.shape
    width = y.shape[1]
    rows, cols = depth // layout.clip_size, width // layout.win_count
    size = layout.size
    half = size["y"] // 2
    pair = added is not None

    def left(y_at, z_at, place_ref):
        return (0, owner_row(layout, place_ref, y_at, z_at))

    def right(j):
        return lambda y_at, z_at, place_ref: (
            0,
            owner_column(layout, place_ref, j, 0 if pair else 1),
        )

    def block(part):
        def index(y_at, z_at, place_ref):
            if part == 0:
                z_at = jnp.where(y_at < half, z_at, size["z"] - 1)
                y_at = jnp.minimum(y_at, half - 1)
            elif part == 1:
                z_at = jnp.where(y_at < half, 0, z_at)
                y_at = jnp.maximum(y_at - half, 0)
            return (y_at, 0, z_at, 0, 0, 0)

        return pl.BlockSpec((1, size["x"], 1, split, rows // split, cols), index)

    out_lead = (half if pair else size["y"], size["x"], size["z"])
    out_shape = jax.ShapeDtypeStruct(out_lead + (split, rows // split, cols), bfloat)
    outs = pl.pallas_call(
        functools.partial(rows_kernel, layout, pair),
        grid_spec=pltpu.PrefetchScalarGridSpec(
            num_scalar_prefetch=1,
            grid=(size["y"], size["z"]),
            in_specs=[pl.BlockSpec((tokens, rows), left)]
            + [pl.BlockSpec((tokens, cols), right(j)) for j in range(size["x"])]
            + [block(None)] * pair,
            out_specs=[block(0), block(1)] if pair else [block(None)],
        ),
        out_shape=[out_shape] * (2 if pair else 1),
        compiler_params=params(),
        cost_estimate=cost(size["x"] * tokens * depth * cols / 382e3),
        name=name,
    )(place, x, *([y] * size["x"]), *([added] if pair else []))
    return Term(outs[0], outs[1], 3) if pair else outs[0]


def to_windows(values, win_count):
    clips, count, width = values.shape
    blocks = GRID // WS
    if win_count == blocks:
        own = values.reshape(clips, FRAMES, WS, blocks, WS, width)
        received = []
        for k in range(blocks - 1, 0, -1):
            pairs = [(w, (w + k) % win_count) for w in range(win_count)]
            received.append((lax.ppermute(own[:, k : k + 1], "win", pairs), 0))
        return [(own, 0), (own, FRAMES - 1)] + received
    halves = win_count // blocks
    wins = blocks // halves
    me = lax.axis_index("win")
    whole = lax.all_gather(values, "win", axis=1, tiled=True)
    whole = whole.reshape(clips, FRAMES, blocks, WS, blocks, WS, width)
    whole = lax.dynamic_slice_in_dim(whole, me // halves, 1, axis=2)
    whole = lax.dynamic_slice_in_dim(whole, (me % halves) * wins, wins, axis=4)
    whole = whole.reshape(clips, FRAMES, WS, wins, WS, width)
    return [(whole, f) for f in range(FRAMES)]


def sent_count(win_count):
    return FRAMES - 2 if win_count == GRID // WS else 0


def send_back(sent, win_count, pin):
    blocks = GRID // WS
    received = []
    for i, array in enumerate(sent):
        k = blocks - 1 - i
        pairs = [((w + k) % win_count, w) for w in range(win_count)]
        received.append(lax.ppermute(array, "win", pairs))
    return tie(received, pin)


def put_together(whole, received, win_count):
    clips, _, _, wins, _, width = whole.shape
    blocks = GRID // WS
    if win_count == blocks:
        for i, array in enumerate(received):
            whole = lax.dynamic_update_slice_in_dim(whole, array, blocks - 1 - i, axis=1)
        return whole.reshape(clips, FRAMES * WS * blocks * WS, width)
    halves = win_count // blocks
    me = lax.axis_index("win")
    whole = lax.all_gather(whole, "win", axis=0, tiled=False)
    whole = whole.reshape(blocks, halves, clips, FRAMES, WS, wins, WS, width)
    whole = whole.transpose(2, 3, 0, 4, 1, 5, 6, 7).reshape(clips, SEQ, width)
    count = SEQ // win_count
    return lax.dynamic_slice_in_dim(whole, me * count, count, axis=1)


def gather_first(arrays, squares, layout):
    me = lax.axis_index("win")
    held, squares = jnp.concatenate([a.reshape(-1) for a in arrays])[None], squares[None]
    win_bits = layout.win_count.bit_length() - 1
    for bit in range(max(win_bits, layout.bits("z"))):
        apart, came, part = layout.win_count >> (bit + 1), held, squares
        if bit < win_bits:
            pairs = [(i, i ^ apart) for i in range(layout.win_count)]
            came = lax.ppermute(held, "win", pairs)
        if bit < layout.bits("z"):
            part = layout.swap(squares, "z", 1 << bit)
        came, part = tie(came, part)
        if bit < win_bits:
            upper = (me & apart) > 0
            first, second = jnp.where(upper, came, held), jnp.where(upper, held, came)
            held = jnp.stack([first, second], axis=1).reshape(2 * held.shape[0], held.shape[1])
        if bit < layout.bits("z"):
            squares = jnp.concatenate([squares, part], axis=0)
    outs, at = [], 0
    for a in arrays:
        outs.append(held[:, at : at + a.size].reshape((layout.win_count,) + a.shape))
        at += a.size
    return outs, squares


def sum_over_win(values, layout):
    me = lax.axis_index("win")
    apart = layout.win_count // 2
    while apart > 0:
        upper = (me & apart) > 0
        first, second = values[:apart], values[apart:]
        sent = jnp.where(upper, first, second)
        kept = jnp.where(upper, second, first)
        pairs = [(i, i ^ apart) for i in range(layout.win_count)]
        values = kept + lax.ppermute(sent, "win", pairs)
        apart //= 2
    return values[0]


def sum_over_clip(values, layout, apart, end):
    while apart < end:
        pairs = [(i, i ^ apart) for i in range(layout.clip_size)]
        values = values + lax.ppermute(values, "clip", pairs)
        apart *= 2
    return values


def local(
    tokens,
    cotangent,
    modulation,
    text_features,
    null_mask,
    null_text,
    norm_gain,
    position_bias,
    self_input,
    self_output,
    cross_query,
    cross_memory,
    cross_output,
    expand_weight,
    reduce_weight,
):
    win_count = lax.axis_size("win")
    clip_size = lax.axis_size("clip")
    layout = Layout(clip_size, win_count)
    place = layout.place()
    blocks = GRID // WS
    clips, _, width = tokens.shape
    hidden_width = reduce_weight.shape[0] * clip_size
    both = ("clip", "win")
    me = lax.axis_index("win")

    input_all = lax.all_gather(self_input, both, axis=0, tiled=False)
    small = [position_bias, norm_gain.astype(single), null_text.astype(single)]
    squares = jnp.concatenate([self_output, cross_query, cross_output, cross_memory], axis=1)
    (bias_full, gain_full, null_full), squares = gather_first(small, squares, layout)
    bias_full = bias_full.reshape(HEADS, NREL)
    pieces = to_windows(tokens, win_count)
    wins = pieces[0][0].shape[3]
    windows = clips * wins
    count = windows * WIN_TOK
    sent = sent_count(win_count)
    columns = width // win_count
    gain_full = gain_full.reshape(1, width)
    null_full = null_full.transpose(1, 0, 2).reshape(TXT, width).astype(bfloat)
    shift = me if win_count == blocks else jnp.int32(0)
    shift = jnp.asarray(shift, jnp.int32).reshape(1)
    blocks_of_bias = table_blocks(bias_full)
    memory_part, squares_part = squares[:, :, 3 * columns :], squares[:, :, : 3 * columns]
    memory_part, blocks_of_bias = layout.gather_axis(memory_part, "y", blocks_of_bias)
    squares_part, blocks_of_bias = layout.gather_axis(squares_part, "x", blocks_of_bias)
    memory_part, squares_part, blocks_of_bias = tie(memory_part, squares_part, blocks_of_bias)
    table = bias_table(blocks_of_bias, shift)
    table, arrays = tie(table, [p[0] for p in pieces])
    pieces = [(array, frame) for array, (_, frame) in zip(arrays, pieces)]
    depth = expand_weight.shape[0]
    feed_shard = jnp.concatenate(
        [expand_weight]
        + [reduce_weight[i : i + depth] for i in range(0, reduce_weight.shape[0], depth)],
        axis=1,
    )
    feed_all = lax.all_gather(feed_shard, both, axis=0, tiled=False)

    token_specs = [piece_spec(wins, width, frame) for _, frame in pieces]
    tokens_in = [array for array, _ in pieces]

    shape = jax.ShapeDtypeStruct
    rows = functools.partial(shape, dtype=bfloat)
    wide = rows((windows, WIN_TOK, width))
    triple = rows((3, windows, WIN_TOK, width))
    triple_spec = pl.BlockSpec((3, 1, WIN_TOK, width), lambda i: (0, i, 0, 0))
    units = rows((3, win_count, windows, WIN_TOK, columns))
    units_spec = pl.BlockSpec((3, win_count, 1, WIN_TOK, columns), lambda i: (0, 0, i, 0, 0))
    wide_single = shape((windows, WIN_TOK, width), single)
    DMA = pltpu.SemaphoreType.DMA

    first_low, projected = pl.pallas_call(
        functools.partial(project_kernel, layout),
        grid=(windows,),
        in_specs=token_specs + [modulation_spec(wins, width), ANY],
        out_specs=[rows_spec(width), rows_spec(3 * width)],
        out_shape=[wide, rows((windows, WIN_TOK, 3 * width))],
        scratch_shapes=[pltpu.VMEM((width, 3 * width), bfloat), DMA(())],
        compiler_params=params(),
        cost_estimate=cost(26),
        name="project",
    )(*tokens_in, modulation, input_all)
    memory_near, memory_far, projected = layout.gather_last(memory_part, "x", projected)
    squares_near, squares_far, projected = layout.gather_last(squares_part, "y", projected)
    memory_all = layout.with_other_core(memory_near, memory_far)
    squares_all = layout.with_other_core(squares_near, squares_far)

    attended, probs = pl.pallas_call(
        attend_kernel,
        grid=(windows,),
        in_specs=[rows_spec(3 * width), BIAS_SPEC],
        out_specs=[rows_spec(width), PROBS_SPEC],
        out_shape=[wide, rows((windows, QUADS, WIN_TOK, LANES))],
        scratch_shapes=[pltpu.VMEM((2, WIN_TOK, LANES), single)],
        compiler_params=params(),
        cost_estimate=cost(37),
        name="attend",
    )(projected, table)

    cotangent, attended = tie(cotangent, attended)
    grad_pieces = to_windows(cotangent, win_count)

    null_flags = null_mask > 0
    used_text = jnp.where(null_flags[:, None, None], null_full[None], text_features)
    text_padded = jnp.pad(used_text, ((0, 0), (0, TEXT_ROWS - TXT), (0, 0)))
    text_spec = pl.BlockSpec((1, TEXT_ROWS, width), lambda i: (i, 0, 0))
    memory = pl.pallas_call(
        functools.partial(memory_kernel, layout),
        grid=(clips,),
        in_specs=[PLACE, text_spec, ANY, ANY, ANY, ANY],
        out_specs=pl.BlockSpec((1, TEXT_ROWS, 2 * width), lambda i: (i, 0, 0)),
        out_shape=rows((clips, TEXT_ROWS, 2 * width)),
        scratch_shapes=[pltpu.VMEM((width, 2 * width), bfloat), DMA(())],
        compiler_params=params(),
        cost_estimate=cost(6),
        name="memory",
    )(place, text_padded, *memory_all)

    gain_spec = pl.BlockSpec((1, width), lambda i: (0, 0))
    memory_spec = pl.BlockSpec((1, TEXT_ROWS, 2 * width), lambda i: (i // wins, 0, 0))
    square = pltpu.VMEM((width, width), bfloat)
    branch, lefts, cross_queries, second_sum = pl.pallas_call(
        functools.partial(cross_kernel, layout),
        grid=(windows,),
        in_specs=[
            PLACE,
            *token_specs,
            rows_spec(width),
            modulation_spec(wins, width),
            gain_spec,
            memory_spec,
            ANY,
            ANY,
            ANY,
            ANY,
        ],
        out_specs=[rows_spec(width), triple_spec, rows_spec(width), rows_spec(width)],
        out_shape=[wide_single, triple, wide, wide_single],
        scratch_shapes=[square, square, square, DMA((3,))],
        compiler_params=params(),
        cost_estimate=cost(42),
        name="cross",
    )(
        place,
        *tokens_in,
        attended,
        modulation,
        gain_full,
        memory,
        *squares_all,
    )

    window_shape = (clips, FRAMES, WS, wins, WS, width)
    piece_shape = (clips, 1, WS, wins, WS, width)
    out_specs = [whole_spec(wins, width)] + [piece_spec(wins, width, 0)] * sent
    out_shapes = [rows(window_shape)] + [rows(piece_shape)] * sent
    feed_out = pl.pallas_call(
        functools.partial(feed_kernel, layout, wins, 1024, sent),
        grid=(windows,),
        in_specs=[piece_spec(wins, width, frame) for _, frame in grad_pieces]
        + [rows_spec(width), modulation_spec(wins, width), ANY],
        out_specs=out_specs
        + [
            rows_spec(width),
            rows_spec(hidden_width),
            rows_spec(hidden_width),
            rows_spec(width),
            rows_spec(width),
            pl.BlockSpec((1, 3, width), lambda i: (i // wins, 0, 0)),
        ],
        out_shape=out_shapes
        + [
            wide,
            rows((windows, WIN_TOK, hidden_width)),
            rows((windows, WIN_TOK, hidden_width)),
            wide,
            wide_single,
            shape((clips, 3, width), single),
        ],
        scratch_shapes=[
            pltpu.VMEM((width, hidden_width), bfloat),
            pltpu.VMEM((hidden_width, width), bfloat),
            DMA((2,)),
        ],
        compiler_params=params(),
        cost_estimate=cost(117),
        name="feed",
    )(*[array for array, _ in grad_pieces], second_sum, modulation, feed_all)
    block_pieces, feed_out = feed_out[: 1 + sent], feed_out[1 + sent :]
    third_low, activated, grad_hidden, grad_reduced, grad_second_sum, feed_mod = feed_out

    def flat(values):
        return values.reshape(-1, count, values.shape[-1])

    def flat_units(values):
        return values.reshape(-1, win_count, count, columns)

    expand_of = (layout, place, flat(third_low), flat(grad_hidden), 1)
    reduce_of = (layout, place, flat(activated)[0], flat(grad_reduced)[0], 4)
    reduce_sent = layout.swap(weight_grad_rows(*reduce_of, None, "reduce_other"), "core", 1)
    expand_sent = layout.swap(weight_grad(*expand_of, None, "expand_other", True, 4), "core", 1)
    reduce_term = weight_grad_rows(*reduce_of, reduce_sent, "reduce_own")
    expand_sent, reduce_term = tie(expand_sent, reduce_term)
    expand_term = weight_grad(*expand_of, expand_sent, "expand_own", True, 4)
    grad_second_sum, expand_term = tie(grad_second_sum, expand_term)

    rights, grad_first_sum, grad_attended, grad_memory, gain_term, gate_mod = pl.pallas_call(
        functools.partial(cross_back_kernel, layout, wins),
        grid=(windows,),
        in_specs=[
            PLACE,
            *token_specs,
            modulation_spec(wins, width),
            gain_spec,
            memory_spec,
            rows_spec(width),
            rows_spec(width),
            rows_spec(width),
            ANY,
            ANY,
            ANY,
            ANY,
        ],
        out_specs=[
            units_spec,
            rows_spec(width),
            rows_spec(width),
            memory_spec,
            gain_spec,
            pl.BlockSpec((1, 1, width), lambda i: (i // wins, 0, 0)),
        ],
        out_shape=[
            units,
            wide_single,
            wide,
            shape((clips, TEXT_ROWS, 2 * width), single),
            shape((1, width), single),
            shape((clips, 1, width), single),
        ],
        scratch_shapes=[square, square, square, DMA((3,))],
        compiler_params=params(),
        cost_estimate=cost(63),
        name="cross_back",
    )(
        place,
        *tokens_in,
        modulation,
        gain_full,
        memory,
        grad_second_sum,
        cross_queries,
        branch,
        *squares_all,
    )
    reduce_stage, grad_attended = layout.reduce_axes([reduce_term], ["y"], grad_attended)
    expand_stage, grad_attended = layout.reduce_axes([expand_term], ["x"], grad_attended)
    rights, grad_memory, reduce_stage, expand_stage = tie(
        rights, grad_memory, reduce_stage, expand_stage
    )

    text_rows = text_padded.reshape(1, clips * TEXT_ROWS, width)
    memory_low = grad_memory.astype(bfloat).reshape(1, clips * TEXT_ROWS, 2 * width)
    square_of = (layout, place, flat(lefts), flat_units(rights), 1)
    memory_of = (layout, place, text_rows, memory_low, 1)
    memory_sent = weight_grad(*memory_of, None, "memory_other", split=2)
    rights, memory_sent = tie(rights, memory_sent)
    memory_sent = layout.swap(memory_sent, "core", 1)
    square_sent = weight_grad(*square_of, None, "square_other")
    masked = jnp.sum(jnp.where(null_flags[:, None, None], grad_memory, 0.0), axis=0)
    square_sent, masked = tie(square_sent, masked)
    square_sent = layout.swap(square_sent, "core", 1)
    null_term = null_text_term(layout, place, masked, memory_all)[:TXT]
    memory_sent, null_term = tie(memory_sent, null_term)
    rest_term = weight_grad(*memory_of, memory_sent, "memory_own", split=2, entries=5)
    square_sent, rest_term = tie(square_sent, rest_term)
    rest_term = weight_grad(
        *square_of, square_sent, "square_own", entries=5, into=rest_term, first=2
    )
    feed_stage, rest_term = layout.reduce_axes([expand_stage, reduce_stage], ["y", "x"], rest_term)
    grad_attended, feed_stage, rest_term, block_pieces = tie(
        grad_attended, feed_stage, rest_term, block_pieces
    )

    grad_projected, bias_sum = pl.pallas_call(
        attend_back_kernel,
        grid=(windows,),
        in_specs=[rows_spec(3 * width), rows_spec(width), PROBS_SPEC],
        out_specs=[units_spec, BIAS_SPEC],
        out_shape=[units, shape((QUADS, WIN_TOK, LANES), single)],
        scratch_shapes=[
            pltpu.VMEM((2, WIN_TOK, LANES), single),
            pltpu.VMEM((2, WIN_TOK, LANES), bfloat),
        ],
        compiler_params=params(),
        cost_estimate=cost(48),
        name="attend_back",
    )(projected, grad_attended, probs)

    feed_stage, bias_sum = layout.reduce([feed_stage], ["z"], [1], bias_sum)
    rest_stage, bias_sum = layout.reduce_axes([rest_term], ["y"], bias_sum)
    block_came, bias_sum = send_back(block_pieces[1:], win_count, bias_sum)
    grad_projected, rest_stage, feed_stage, block_came = tie(
        grad_projected, rest_stage, feed_stage, block_came
    )
    input_of = (layout, place, flat(first_low), flat_units(grad_projected), 3)
    input_sent = weight_grad(*input_of, None, "input_other", True, 3)
    input_sent = layout.swap(input_sent, "core", 1)
    input_term = weight_grad(*input_of, input_sent, "input_own", True, 3)
    bias_sum, input_term = tie(bias_sum, input_term)
    position_flat = bias_blocks(bias_sum, shift)
    for bit in range(1, layout.bits("z")):
        feed_stage, position_flat = layout.reduce([feed_stage], ["z"], [1 << bit], position_flat)
    rest_stage, position_flat = layout.reduce_axes([rest_stage], ["x"], position_flat)
    position_term = bias_collect(position_flat)
    grad_projected, rest_stage, feed_grad, position_term = tie(
        grad_projected, rest_stage, feed_stage, position_term
    )

    input_out = pl.pallas_call(
        functools.partial(input_back_kernel, layout, wins, sent),
        grid=(windows,),
        in_specs=token_specs + [modulation_spec(wins, width), units_spec, rows_spec(width), ANY],
        out_specs=out_specs + [pl.BlockSpec((1, 2, width), lambda i: (i // wins, 0, 0))],
        out_shape=out_shapes + [shape((clips, 2, width), single)],
        scratch_shapes=[pltpu.VMEM((width, 3 * width), bfloat), DMA(())],
        compiler_params=params(),
        cost_estimate=cost(29),
        name="input_back",
    )(*tokens_in, modulation, grad_projected, grad_first_sum, input_all)
    first_mod = input_out[-1]
    input_stage, first_mod = layout.reduce_axes([input_term], ["x"], first_mod)
    input_stage, first_mod = tie(input_stage, first_mod)
    rest_came, first_mod = layout.exchange([rest_stage], ["z"], [1], first_mod)
    expand_grad = jnp.concatenate(list(feed_grad[:4]), axis=1)
    reduce_grad = feed_grad[4:].reshape(4 * depth, columns)
    heads_local = HEADS // win_count
    modulation_term = jnp.concatenate([first_mod, gate_mod, feed_mod], axis=1)
    by_columns = jnp.concatenate(
        [modulation_term.reshape(clips * 6, width), gain_term, null_term], axis=0
    )
    by_columns = by_columns.reshape(-1, win_count, columns).transpose(1, 0, 2)
    small_term = jnp.concatenate(
        [
            by_columns.reshape(win_count, -1),
            position_term.reshape(win_count, heads_local * NREL),
        ],
        axis=1,
    )
    small_term = sum_over_win(small_term, layout)
    block_whole, block_came, small_term = tie(block_pieces[0], block_came, small_term)
    block_output = put_together(block_whole, block_came, win_count)
    rest_came, small_term = tie(rest_came, small_term)
    rest_stage = layout.combine([rest_stage], rest_came)
    input_stage, small_term = layout.reduce_axes([input_stage], ["y"], small_term)
    modulation_grad = small_term[: clips * 6 * columns].reshape(clips, 6, columns)
    small_grad = sum_over_clip(small_term[clips * 6 * columns :], layout, 1, clip_size // 2)
    for bit in range(1, layout.bits("z")):
        rest_stage, small_grad = layout.reduce([rest_stage], ["z"], [1 << bit], small_grad)
    input_stage, small_grad = layout.reduce([input_stage], ["z"], [1], small_grad)
    input_stage, small_grad = tie(input_stage, small_grad)
    tokens_came, small_grad = send_back(input_out[1 : 1 + sent], win_count, small_grad)
    tokens_grad = put_together(input_out[0], tokens_came, win_count)
    small_grad = sum_over_clip(small_grad, layout, clip_size // 2, clip_size)
    gain_grad = small_grad[:columns]
    null_grad = small_grad[columns : (1 + TXT) * columns].reshape(TXT, columns)
    position_grad = small_grad[(1 + TXT) * columns :].reshape(heads_local, NREL)
    for bit in range(1, layout.bits("z")):
        input_stage, small_grad = layout.reduce([input_stage], ["z"], [1 << bit], small_grad)
    cross_memory_grad = jnp.concatenate([rest_stage[0], rest_stage[1]], axis=1)
    self_input_grad = jnp.concatenate(list(input_stage), axis=1)
    self_output_grad, cross_query_grad, cross_output_grad = rest_stage[2:]
    return (
        block_output,
        tokens_grad,
        self_input_grad,
        self_output_grad,
        cross_query_grad,
        cross_memory_grad,
        cross_output_grad,
        expand_grad,
        reduce_grad,
        gain_grad,
        null_grad,
        position_grad,
        modulation_grad,
    )


def solution(mesh):
    in_specs = (
        P("clip", "win", None),
        P("clip", "win", None),
        P("clip", None, None),
        P("clip", None, None),
        P("clip"),
        P(None, "win"),
        P("win"),
        P("win", None),
        P("clip", "win"),
        P("clip", "win"),
        P("clip", "win"),
        P("clip", "win"),
        P("clip", "win"),
        P("clip", "win"),
        P("clip", "win"),
    )
    out_specs = (
        P("clip", "win", None),
        P("clip", "win", None),
        P("clip", "win"),
        P("clip", "win"),
        P("clip", "win"),
        P("clip", "win"),
        P("clip", "win"),
        P("clip", "win"),
        P("clip", "win"),
        P("win"),
        P(None, "win"),
        P("win", None),
        P("clip", None, "win"),
    )
    return jax.shard_map(local, mesh=mesh, in_specs=in_specs, out_specs=out_specs, check_vma=False)
```
